32 devices in a mesh: user: 8 (over z, core), item: 4 (over y, x).
Axes of the slice: x: 2, y: 2, z: 4, core: 2. Of those that a mesh axis runs over, the one named last changes fastest.
Arguments:
- user_factors: float32 [4096, 256], P('user'), may hold values from -0.3 to 0.3, as said below
- item_factors: float32 [2048, 256], P('item'), may hold values from -0.6 to 0.6
- tile_user: int32 [4, 8, 8, 2], P('item', 'user'), may hold values from 0 to 3
- tile_item: int32 [4, 8, 8, 2], P('item', 'user'), may hold values from 0 to 3
- tile_count: int32 [4, 8, 8], P('item', 'user'), may hold values from 1 to 2, as said below
- tile_conf: bfloat16 [4, 8, 8, 2, 128, 128], P('item', 'user'), may hold values from 0.099609375 to 4
- held_user: int32 [8, 4, 4, 2], P('user', 'item'), may hold values from 0 to 1
- held_item: int32 [8, 4, 4, 2], P('user', 'item'), may hold values from 0 to 3
- held_count: int32 [8, 4, 4], P('user', 'item'), may hold values from 1 to 2, as said below
- held_conf: bfloat16 [8, 4, 4, 2, 128, 128], P('user', 'item'), may hold values from 0.099609375 to 4
Outputs:
- new_items: float32 [2048, 256], P('item')
- folded_users: float32 [2048, 256], P('user')
The draws below stay inside these ranges and needn't reach their ends.
Inputs may be any that keep to these rules, and one draw needn't show every extreme that they name: `user_factors`: user factors; the scale of a factor column varies by up to a factor of ten. `tile_count`: some device has an owner with all 2 slots live and one with a single live slot. `held_count`: some device has an owner with all 2 slots live and one with a single live slot.
All inputs are finite; a program needn't handle non-finite values.
Results may differ from the reference program's by a relative error of at most 0.0003.
Values may be sent and summed in bfloat16 or wider, within the bound.
A program may use at most 128 MiB of HBM per device.

```python
import math
import jax
import jax.numpy as jnp
from jax import lax

K = 256
BL = 128
UB_DEV = 4
IB_DEV = 4
HB_DEV = 2
CAP = 2
HCAP = 2
ITERS = 2
USERS = 4096
ITEMS = 2048
HELD = 2048
N_USER = 8
N_ITEM = 4


def draw_user_factors(key, part):
    scale_key, value_key = jax.random.split(jax.random.fold_in(key, 7))
    scales = jnp.exp(jax.random.uniform(scale_key, (K,), jnp.float32, 0.0, math.log(10.0)))
    values = jax.random.uniform(value_key, (USERS, K), jnp.float32, -1.0, 1.0)
    return values * scales[None, :] * 0.03


def draw_tile_count(key, part):
    counts = jax.random.randint(jax.random.fold_in(key, 3), (N_ITEM, N_USER, N_USER), 1, CAP + 1)
    counts = counts.at[0, 0, 0].set(CAP)
    return counts.at[0, 0, 1].set(1)


def draw_held_count(key, part):
    counts = jax.random.randint(jax.random.fold_in(key, 5), (N_USER, N_ITEM, N_ITEM), 1, HCAP + 1)
    counts = counts.at[0, 0, 0].set(HCAP)
    return counts.at[0, 0, 1].set(1)


def set_ends(array, stream_key, smallest, high):
    longest = array.shape.index(max(array.shape))
    spots = []
    for shift in (0, 1):
        where = [jax.random.randint(jax.random.fold_in(stream_key, axis), (), 0, length) for axis, length in enumerate(array.shape)]
        where[longest] = (where[longest] + shift) % array.shape[longest]
        spots.append(tuple(where))
    return array.at[spots[0]].set(smallest).at[spots[1]].set(high)


def steps_of(own_key, extent, shards, least, top_value):
    loudness = 1.0
    for dim, blocks in shards:
        steps = jax.random.uniform(jax.random.fold_in(jax.random.fold_in(own_key, 6), dim), (blocks,), jnp.float32, least / len(shards), top_value / len(shards))
        loudness = loudness * jnp.repeat(jnp.exp(steps), extent[dim] // blocks).reshape((-1,) + (1,) * (len(extent) - 1 - dim))
    return loudness


def noise(rng, extent, spread, limit, cuts=(), kind=jnp.bfloat16):
    loudness = steps_of(rng, extent, cuts, -0.22, 0.18) if cuts else 1.0
    array = jax.random.normal(rng, extent, jnp.float32) * spread * loudness
    return jnp.minimum(jnp.maximum(array, -limit), limit).astype(kind)


def setup_inputs(seed: int = 0) -> dict:
    streams_of = jax.random.split(jax.random.key(seed), 11)
    user_factors = draw_user_factors(jax.random.fold_in(streams_of[10], 71), 0)
    item_factors = noise(streams_of[1], (ITEMS, K), 0.1, 0.6, ((0, 4),), jnp.float32)
    tile_user = set_ends(jax.random.randint(streams_of[2], (N_ITEM, N_USER, N_USER, CAP), 0, UB_DEV), jax.random.fold_in(streams_of[2], 1), 0, UB_DEV - 1).astype(jnp.int32)
    tile_item = set_ends(jax.random.randint(streams_of[3], (N_ITEM, N_USER, N_USER, CAP), 0, IB_DEV), jax.random.fold_in(streams_of[3], 1), 0, IB_DEV - 1).astype(jnp.int32)
    tile_count = draw_tile_count(jax.random.fold_in(streams_of[10], 71), 0)
    tile_conf = jnp.clip(jnp.exp(math.log(4.0) - 3.6927934 * jax.random.uniform(streams_of[5], (N_ITEM, N_USER, N_USER, CAP, BL, BL), jnp.float32) ** steps_of(streams_of[5], (N_ITEM, N_USER, N_USER, CAP, BL, BL), ((0, 4), (1, 8)), -0.2, 0.2)), 0.099609375, 4.0).astype(jnp.bfloat16)
    held_user = set_ends(jax.random.randint(streams_of[6], (N_USER, N_ITEM, N_ITEM, HCAP), 0, HB_DEV), jax.random.fold_in(streams_of[6], 1), 0, HB_DEV - 1).astype(jnp.int32)
    held_item = set_ends(jax.random.randint(streams_of[7], (N_USER, N_ITEM, N_ITEM, HCAP), 0, IB_DEV), jax.random.fold_in(streams_of[7], 1), 0, IB_DEV - 1).astype(jnp.int32)
    held_count = draw_held_count(jax.random.fold_in(streams_of[10], 71), 0)
    held_conf = jnp.clip(jnp.exp(math.log(4.0) - 3.6927934 * jax.random.uniform(streams_of[9], (N_USER, N_ITEM, N_ITEM, HCAP, BL, BL), jnp.float32) ** steps_of(streams_of[9], (N_USER, N_ITEM, N_ITEM, HCAP, BL, BL), ((0, 8), (1, 4)), -0.2, 0.2)), 0.099609375, 4.0).astype(jnp.bfloat16)
    return dict(user_factors=user_factors, item_factors=item_factors, tile_user=tile_user, tile_item=tile_item, tile_count=tile_count, tile_conf=tile_conf, held_user=held_user, held_item=held_item, held_count=held_count, held_conf=held_conf)


highest = lax.Precision.HIGHEST
ridge_weight = 1.0
epsilon = 1e-6


def local_gram(rows):
    return jnp.einsum('nk,nm->km', rows, rows, precision=highest)


def gram_apply(vector, gram):
    return jnp.einsum('jck,km->jcm', vector, gram, precision=highest) + ridge_weight * vector


def block_onehot(positions, blocks):
    return (positions[:, None] == jnp.arange(blocks, dtype=jnp.int32)[None, :]).astype(jnp.float32)


def item_terms(factors, weights, positions, onehot, vector):
    picked = vector[positions]
    scores = jnp.einsum('tuk,tik->tui', factors, picked, precision=highest) * weights
    terms = jnp.einsum('tui,tuk->tik', scores, factors, precision=highest)
    return jnp.einsum('tj,tik->jik', onehot, terms, precision=highest)


def item_right(factors, right_weights, onehot):
    terms = jnp.einsum('tui,tuk->tik', right_weights, factors, precision=highest)
    return jnp.einsum('tj,tik->jik', onehot, terms, precision=highest)


def held_terms(factors, weights, positions, onehot, vector):
    picked = vector[positions]
    scores = jnp.einsum('tik,thk->thi', factors, picked, precision=highest) * weights
    terms = jnp.einsum('thi,tik->thk', scores, factors, precision=highest)
    return jnp.einsum('tj,thk->jhk', onehot, terms, precision=highest)


def held_right(factors, right_weights, onehot):
    terms = jnp.einsum('thi,tik->thk', right_weights, factors, precision=highest)
    return jnp.einsum('tj,thk->jhk', onehot, terms, precision=highest)


def conjugate(operator, residual, start):
    solution = start
    direction = residual
    norm_now = jnp.sum(residual * residual, axis=-1, keepdims=True)
    for iteration in range(ITERS):
        image = operator(direction)
        alpha = norm_now / (jnp.sum(direction * image, axis=-1, keepdims=True) + epsilon)
        solution = solution + alpha * direction
        residual = residual - alpha * image
        norm_next = jnp.sum(residual * residual, axis=-1, keepdims=True)
        direction = residual + (norm_next / (norm_now + epsilon)) * direction
        norm_now = norm_next
    return solution


def reference(user_factors, item_factors, tile_user, tile_item, tile_count, tile_conf, held_user, held_item, held_count, held_conf):
    gram_users = local_gram(user_factors)
    user_blocks = user_factors.reshape(N_USER * UB_DEV, BL, K)
    user_owner = jnp.arange(N_USER, dtype=jnp.int32)[:, None] * UB_DEV

    def item_shard(packed):
        user_index, item_index, tile_counts, confidence, warm_start = packed
        named_blocks = (user_owner + user_index).reshape(-1)
        factors = user_blocks[named_blocks]
        live_flat = (jnp.arange(CAP, dtype=jnp.int32)[None, None, :] < tile_counts[:, :, None]).astype(jnp.float32).reshape(-1)[:, None, None]
        conf_flat = confidence.reshape(-1, BL, BL).astype(jnp.float32)
        weights = conf_flat * live_flat
        right_weights = (1.0 + conf_flat) * live_flat
        positions = item_index.reshape(-1)
        onehot = block_onehot(positions, IB_DEV)
        start_blocks = warm_start.reshape(IB_DEV, BL, K)

        def operator(direction):
            return item_terms(factors, weights, positions, onehot, direction) + gram_apply(direction, gram_users)

        residual = item_right(factors, right_weights, onehot) - operator(start_blocks)
        return conjugate(operator, residual, start_blocks).reshape(IB_DEV * BL, K)

    new_items = lax.map(item_shard, (tile_user, tile_item, tile_count, tile_conf, item_factors.reshape(N_ITEM, IB_DEV * BL, K))).reshape(ITEMS, K)

    gram_items = local_gram(new_items)
    item_blocks = new_items.reshape(N_ITEM * IB_DEV, BL, K)
    item_owner = jnp.arange(N_ITEM, dtype=jnp.int32)[:, None] * IB_DEV

    def held_shard(packed):
        held_index, owner_index, held_counts, confidence = packed
        named_blocks = (item_owner + owner_index).reshape(-1)
        factors = item_blocks[named_blocks]
        live_flat = (jnp.arange(HCAP, dtype=jnp.int32)[None, None, :] < held_counts[:, :, None]).astype(jnp.float32).reshape(-1)[:, None, None]
        conf_flat = confidence.reshape(-1, BL, BL).astype(jnp.float32)
        weights = conf_flat * live_flat
        right_weights = (1.0 + conf_flat) * live_flat
        positions = held_index.reshape(-1)
        onehot = block_onehot(positions, HB_DEV)

        def operator(direction):
            return held_terms(factors, weights, positions, onehot, direction) + gram_apply(direction, gram_items)

        residual = held_right(factors, right_weights, onehot)
        zero_start = jnp.zeros((HB_DEV, BL, K), jnp.float32)
        return conjugate(operator, residual, zero_start).reshape(HB_DEV * BL, K)

    folded_users = lax.map(held_shard, (held_user, held_item, held_count, held_conf)).reshape(HELD, K)
    return new_items, folded_users
```

```python
import functools

import jax
import jax.numpy as jnp
from jax import lax
from jax.experimental import pallas as pl
from jax.experimental.pallas import tpu as pltpu
from jax.sharding import PartitionSpec as P

ITERS = 2
RIDGE = 1.0
EPS = 1e-6
MESH = pl.DeviceIdType.MESH
ANY = pl.BlockSpec(memory_space=pl.ANY)
VMEM = pl.BlockSpec(memory_space=pltpu.VMEM)
SMEM = pl.BlockSpec(memory_space=pltpu.SMEM)


def place(users, items):
    u = lax.axis_index("user")
    return lax.axis_index("item"), u, u // 2, lax.rem(u, 2)


def greet(devices):
    barrier = pltpu.get_barrier_semaphore()
    for device in devices:
        pl.semaphore_signal(barrier, inc=1, device_id=device, device_id_type=MESH)
    pl.semaphore_wait(barrier, len(devices))


def send(src, dst, send_sem, recv_sem, device):
    copy = pltpu.make_async_remote_copy(
        src_ref=src, dst_ref=dst, send_sem=send_sem, recv_sem=recv_sem, device_id=device, device_id_type=MESH
    )
    copy.start()
    return copy


def pack_rows(tile_of, out, slots, peers):
    rows = out.shape[1] // slots
    group = max(1, 16 // rows)
    for first in range(0, slots, group):
        tiles = [tile_of(first + k) for k in range(group)]
        for p in range(peers):
            part = [t[p * rows:(p + 1) * rows] for t in tiles]
            part = part[0] if group == 1 else jnp.concatenate(part, axis=0)
            out[p, first * rows:(first + group) * rows, :] = part.astype(out.dtype)


def spread_kernel(users, items, y_ref, conf_ref, held_ref, meta_ref,
                  y_out, c_out, h_out, mu_out, mi_out, c_send, h_send,
                  z_s, z_r, xy_s, xy_r, sib_s, sib_r, own_s, own_r,
                  c_s, c_r, h_s, h_r, mu_s, mu_r, mi_s, mi_r, local):
    zs = users // 2
    i, u, z, c = place(users, items)
    sibling = (2 * z + 1 - c, i)
    quarter = y_ref.shape[1]
    user_peers = [lax.rem(u + k, users) for k in range(1, users)]
    item_peers = [lax.rem(i + e, items) for e in range(1, items)]
    greet([(p, i) for p in user_peers] + [(u, p) for p in item_peers])

    pending = []
    crossing = []
    for d in range(1, zs):
        peer = 2 * lax.rem(z + d, zs) + c
        crossing.append(send(y_ref.at[i], y_out.at[u, i], z_s.at[d], z_r.at[d], (peer, i)))
    pending.append(send(y_ref, y_out.at[u], own_s, own_r, sibling))
    keep = [pltpu.make_async_copy(y_ref, y_out.at[u], local.at[0])]
    keep[0].start()
    for k, p in enumerate(user_peers):
        pending.append(send(meta_ref, mu_out.at[u], mu_s.at[k], mu_r.at[k], (p, i)))
    for e, p in enumerate(item_peers):
        pending.append(send(meta_ref, mi_out.at[i], mi_s.at[e], mi_r.at[e], (u, p)))

    slots = conf_ref.shape[0]
    pack_rows(lambda s: conf_ref[s].astype(jnp.float32).T, c_send, slots, users)
    for k, p in enumerate(user_peers):
        pending.append(send(c_send.at[p], c_out.at[u], c_s.at[k], c_r.at[k], (p, i)))
    held_slots = held_ref.shape[0]
    pack_rows(lambda s: held_ref[s].astype(jnp.float32), h_send, held_slots, items)
    for e, p in enumerate(item_peers):
        pending.append(send(h_send.at[p], h_out.at[i], h_s.at[e], h_r.at[e], (u, p)))
    keep.append(pltpu.make_async_copy(c_send.at[u], c_out.at[u], local.at[1]))
    keep.append(pltpu.make_async_copy(h_send.at[i], h_out.at[i], local.at[2]))
    keep.append(pltpu.make_async_copy(meta_ref, mu_out.at[u], local.at[3]))
    keep.append(pltpu.make_async_copy(meta_ref, mi_out.at[i], local.at[4]))
    for copy in keep[1:]:
        copy.start()

    across = {}
    for d in range(1, zs):
        crossing[d - 1].wait_recv()
        shard = 2 * lax.rem(z - d + zs, zs) + c
        block = y_out.at[shard, i]
        for e, p in enumerate(item_peers):
            across[d, e] = send(block, block, xy_s.at[d, e], xy_r.at[d, e], (u, p))
        pending.append(send(block, block, sib_s.at[d, items - 1], sib_r.at[d, items - 1], sibling))
    for d in range(1, zs):
        shard = 2 * lax.rem(z - d + zs, zs) + c
        for e in range(items - 1):
            across[d, e].wait_recv()
            block = y_out.at[shard, lax.rem(i - e - 1 + items, items)]
            pending.append(send(block, block, sib_s.at[d, e], sib_r.at[d, e], sibling))
    for copy in crossing + list(across.values()):
        copy.wait_send()
    for copy in pending:
        copy.wait()
    for copy in keep:
        copy.wait()


def spread(users, items, factors, conf, held, meta):
    rows, rank = factors.shape
    slots, width = conf.shape[0], conf.shape[1]
    held_slots = held.shape[0]
    zs = users // 2
    c_piece = (slots * width // users, width)
    h_piece = (held_slots * width // items, width)
    dma = pltpu.SemaphoreType.DMA
    return pl.pallas_call(
        functools.partial(spread_kernel, users, items),
        out_shape=[
            jax.ShapeDtypeStruct((users, items, rows // items, rank), jnp.float32),
            jax.ShapeDtypeStruct((users,) + c_piece, jnp.bfloat16),
            jax.ShapeDtypeStruct((items,) + h_piece, jnp.bfloat16),
            jax.ShapeDtypeStruct((users,) + meta.shape, jnp.int32),
            jax.ShapeDtypeStruct((items,) + meta.shape, jnp.int32),
        ],
        in_specs=[ANY, VMEM, VMEM, VMEM],
        out_specs=[ANY] * 5,
        scratch_shapes=[
            pltpu.VMEM((users,) + c_piece, jnp.bfloat16),
            pltpu.VMEM((items,) + h_piece, jnp.bfloat16),
            dma((zs,)), dma((zs,)), dma((zs, items)), dma((zs, items)), dma((zs, items)), dma((zs, items)),
            dma, dma, dma((users,)), dma((users,)), dma((items,)), dma((items,)),
            dma((users,)), dma((users,)), dma((items,)), dma((items,)), dma((5,)),
        ],
        compiler_params=pltpu.CompilerParams(
            collective_id=0, has_side_effects=True, vmem_limit_bytes=16 * 2**20
        ),
        name="spread_inputs",
    )(factors.reshape(items, rows // items, rank), conf, held, meta)


def halves(value):
    high = value.astype(jnp.bfloat16)
    return high, (value - high.astype(jnp.float32)).astype(jnp.bfloat16)


def dot(a, b, contract):
    return lax.dot_general(a, b, (((1,), (contract,)), ((), ())), preferred_element_type=jnp.float32)


def product(value, high, low, contract):
    n = value.shape[0]
    top, bottom = halves(value)
    both = dot(jnp.concatenate([top, bottom], axis=0), high, contract)
    return both[:n] + both[n:] + dot(top, low, contract)


def solve_kernel(warm, by_owner, codes_ref, table_ref, tiles_ref, *rest):
    if warm:
        start_ref, out_ref, high, low, weight, right = rest
    else:
        out_ref, high, low, weight, right = rest
    blocks, rows, width = weight.shape
    sources, piece = tiles_ref.shape[0], tiles_ref.shape[1]
    rank = table_ref.shape[1]
    slots = codes_ref.shape[1]
    part = piece // slots
    cap = slots // by_owner
    per_owner = blocks // by_owner
    chunk = 4
    span = chunk * width

    def prepare(b, carry):
        weight[b] = jnp.ones((rows, width), jnp.float32)
        right[b] = jnp.zeros((rows, width), jnp.float32)
        at = pl.ds(pl.multiple_of(b * width, width), width)
        top, bottom = halves(table_ref[at, :])
        high[at, :] = top
        low[at, :] = bottom
        return carry

    lax.fori_loop(0, blocks, prepare, 0)

    def place_tiles(source, carry):
        for s in range(slots):
            code = codes_ref[source, s]

            @pl.when(code >= 0)
            def _():
                block = (s // cap) * per_owner + lax.rem(code, per_owner)
                at = pl.ds(pl.multiple_of((code // per_owner) * part, part), part)
                tile = tiles_ref[source, s * part:(s + 1) * part, :].astype(jnp.float32)
                weight[block, at, :] += tile
                right[block, at, :] += tile + 1.0

        return carry

    lax.fori_loop(0, sources, place_tiles, 0)

    def wide(ref, n):
        return jnp.concatenate([ref[n * chunk + k] for k in range(chunk)], axis=1)

    def sweep(coefficients):
        def step(n, total):
            at = pl.ds(pl.multiple_of(n * span, span), span)
            top, bottom = high[at, :], low[at, :]
            return total + product(coefficients(n, top, bottom), top, bottom, 0)

        return lax.fori_loop(0, blocks // chunk, step, jnp.zeros((rows, rank), jnp.float32), unroll=2)

    def operator(vector):
        return sweep(lambda n, top, bottom: product(vector, top, bottom, 1) * wide(weight, n)) + RIDGE * vector

    if warm:
        x = start_ref[...]
        residual = sweep(
            lambda n, top, bottom: wide(right, n) - product(x, top, bottom, 1) * wide(weight, n)
        ) - RIDGE * x
    else:
        x = jnp.zeros((rows, rank), jnp.float32)
        residual = sweep(lambda n, top, bottom: wide(right, n))
    direction = residual
    norm = jnp.sum(residual * residual, axis=1, keepdims=True)
    for iteration in range(ITERS):
        image = operator(direction)
        alpha = norm / (jnp.sum(direction * image, axis=1, keepdims=True) + EPS)
        x = x + alpha * direction
        if iteration + 1 < ITERS:
            residual = residual - alpha * image
            following = jnp.sum(residual * residual, axis=1, keepdims=True)
            direction = residual + following / (norm + EPS) * direction
            norm = following
    out_ref[...] = x


def solve(codes, table, tiles, rows, by_owner, start=None):
    width = tiles.shape[2]
    count, rank = table.shape
    blocks = count // width
    warm = start is not None
    args = [codes, table, tiles] + ([start] if warm else [])
    return pl.pallas_call(
        functools.partial(solve_kernel, warm, by_owner),
        out_shape=jax.ShapeDtypeStruct((rows, rank), jnp.float32),
        in_specs=[SMEM] + [VMEM] * (len(args) - 1),
        out_specs=VMEM,
        scratch_shapes=[
            pltpu.VMEM((count, rank), jnp.bfloat16),
            pltpu.VMEM((count, rank), jnp.bfloat16),
            pltpu.VMEM((blocks, rows, width), jnp.float32),
            pltpu.VMEM((blocks, rows, width), jnp.float32),
        ],
        compiler_params=pltpu.CompilerParams(vmem_limit_bytes=40 * 2**20),
        name="solve_items" if warm else "solve_held",
    )(*args)


def gather_items_kernel(users, items, x_ref, x_out, z_s, z_r, xy_s, xy_r, sib_s, sib_r, local):
    zs = users // 2
    i, u, z, c = place(users, items)
    sibling = (2 * z + 1 - c, i)
    z_peers = [2 * lax.rem(z + d, zs) + c for d in range(1, zs)]
    item_peers = [lax.rem(i + e, items) for e in range(1, items)]
    greet([(p, i) for p in z_peers] + [(u, p) for p in item_peers] + [sibling])

    crossing, across, pending = [], {}, []
    own = x_out.at[i, :, u]
    for d, p in enumerate(z_peers):
        crossing.append(send(x_ref, own, z_s.at[d], z_r.at[d], (p, i)))
    for e, p in enumerate(item_peers):
        across[0, e] = send(x_ref, own, xy_s.at[0, e], xy_r.at[0, e], (u, p))
    pending.append(send(x_ref, own, sib_s.at[0, items - 1], sib_r.at[0, items - 1], sibling))
    keep = pltpu.make_async_copy(x_ref, own, local)
    keep.start()
    for d in range(1, zs):
        crossing[d - 1].wait_recv()
        block = x_out.at[i, :, 2 * lax.rem(z - d + zs, zs) + c]
        for e, p in enumerate(item_peers):
            across[d, e] = send(block, block, xy_s.at[d, e], xy_r.at[d, e], (u, p))
        pending.append(send(block, block, sib_s.at[d, items - 1], sib_r.at[d, items - 1], sibling))
    for d in range(zs):
        shard = 2 * lax.rem(z - d + zs, zs) + c
        for e in range(items - 1):
            across[d, e].wait_recv()
            block = x_out.at[lax.rem(i - e - 1 + items, items), :, shard]
            pending.append(send(block, block, sib_s.at[d, e], sib_r.at[d, e], sibling))
    for copy in crossing + list(across.values()):
        copy.wait_send()
    for copy in pending:
        copy.wait()
    keep.wait()


def gather_items(users, items, piece):
    blocks, part, rank = piece.shape
    zs = users // 2
    dma = pltpu.SemaphoreType.DMA
    return pl.pallas_call(
        functools.partial(gather_items_kernel, users, items),
        out_shape=jax.ShapeDtypeStruct((items, blocks, users, part, rank), jnp.float32),
        in_specs=[ANY],
        out_specs=ANY,
        scratch_shapes=[dma((zs,)), dma((zs,))] + [dma((zs, items))] * 4 + [dma],
        compiler_params=pltpu.CompilerParams(
            collective_id=1, has_side_effects=True, vmem_limit_bytes=16 * 2**20
        ),
        name="gather_items",
    )(piece)


def gather_held_kernel(users, items, f_ref, f_out, s_sem, r_sem, local):
    i, u, z, c = place(users, items)
    item_peers = [lax.rem(i + e, items) for e in range(1, items)]
    greet([(u, p) for p in item_peers])
    own = f_out.at[:, i]
    copies = [send(f_ref, own, s_sem.at[e], r_sem.at[e], (u, p)) for e, p in enumerate(item_peers)]
    keep = pltpu.make_async_copy(f_ref, own, local)
    keep.start()
    for copy in copies:
        copy.wait()
    keep.wait()


def gather_held(users, items, piece):
    blocks, part, rank = piece.shape
    dma = pltpu.SemaphoreType.DMA
    return pl.pallas_call(
        functools.partial(gather_held_kernel, users, items),
        out_shape=jax.ShapeDtypeStruct((blocks, items, part, rank), jnp.float32),
        in_specs=[ANY],
        out_specs=ANY,
        scratch_shapes=[dma((items,)), dma((items,)), dma],
        compiler_params=pltpu.CompilerParams(
            collective_id=2, has_side_effects=True, vmem_limit_bytes=16 * 2**20
        ),
        name="gather_held",
    )(piece)


def slot_codes(joined, named, counts, per_owner):
    slots = joined.shape[1]
    live = jnp.arange(slots, dtype=jnp.int32)[None, :] < counts[:, None]
    return jnp.where(live, joined * per_owner + named, -1).reshape(1, -1)


def shards(user_factors, item_factors, tile_user, tile_item, tile_count, tile_conf,
           held_user, held_item, held_count, held_conf):
    users, items = lax.axis_size("user"), lax.axis_size("item")
    width = tile_conf.shape[-1]
    rank = user_factors.shape[1]
    user_blocks = user_factors.shape[0] // width
    item_blocks = item_factors.shape[0] // width
    held_blocks = 2
    u = lax.axis_index("user")
    i = lax.axis_index("item")

    codes = slot_codes(tile_item[0, 0], tile_user[0, 0], tile_count[0, 0], user_blocks)
    held_codes = slot_codes(held_user[0, 0], held_item[0, 0], held_count[0, 0], item_blocks)
    slots, held_slots = codes.shape[1], held_codes.shape[1]
    lanes = -(-max(slots, held_slots) // 128) * 128
    meta = jnp.concatenate([
        jnp.pad(codes, ((0, 0), (0, lanes - slots))),
        jnp.pad(held_codes, ((0, 0), (0, lanes - held_slots))),
        jnp.zeros((6, lanes), jnp.int32),
    ], axis=0)
    conf = tile_conf.reshape(-1, width, width)
    held = held_conf.reshape(-1, width, width)
    table, tiles, held_tiles, user_meta, item_meta = spread(users, items, user_factors, conf, held, meta)

    part = width // users
    start = lax.dynamic_index_in_dim(
        item_factors.reshape(item_blocks, users, part, rank), u, axis=1, keepdims=False
    ).reshape(-1, rank)
    own = solve(user_meta[:, 0, :slots], table.reshape(-1, rank), tiles, item_blocks * part, users, start)
    whole = gather_items(users, items, own.reshape(item_blocks, part, rank))
    new_items = lax.dynamic_index_in_dim(whole, i, axis=0, keepdims=False).reshape(-1, rank)

    held_part = width // items
    folded = solve(item_meta[:, 1, :held_slots], whole.reshape(-1, rank), held_tiles, held_blocks * held_part, items)
    folded_users = gather_held(users, items, folded.reshape(held_blocks, held_part, rank))
    return new_items, folded_users.reshape(-1, rank)


def solution(mesh):
    in_specs = (
        P("user", None),
        P("item", None),
        P("item", "user", None, None),
        P("item", "user", None, None),
        P("item", "user", None),
        P("item", "user", None, None, None, None),
        P("user", "item", None, None),
        P("user", "item", None, None),
        P("user", "item", None),
        P("user", "item", None, None, None, None),
    )
    out_specs = (P("item", None), P("user", None))
    return jax.shard_map(shards, mesh=mesh, in_specs=in_specs, out_specs=out_specs, check_vma=False)
```

```python
import functools

import jax
import jax.numpy as jnp
from jax import lax
from jax.experimental import pallas as pl
from jax.experimental.pallas import tpu as pltpu
from jax.sharding import PartitionSpec as P

ITERS = 2
RIDGE = 1.0
EPS = 1e-6
MESH = pl.DeviceIdType.MESH
ANY = pl.BlockSpec(memory_space=pl.ANY)
VMEM = pl.BlockSpec(memory_space=pltpu.VMEM)
HBM = pl.BlockSpec(memory_space=pltpu.HBM)
SMEM = pl.BlockSpec(memory_space=pltpu.SMEM)


def place(users, items):
    u = lax.axis_index("user")
    return lax.axis_index("item"), u, u // 2, lax.rem(u, 2)


def greet(devices):
    for device in devices:
        pl.semaphore_signal(pltpu.get_barrier_semaphore(), inc=1, device_id=device, device_id_type=MESH)


def await_greetings(devices):
    pl.semaphore_wait(pltpu.get_barrier_semaphore(), len(devices))


def send(src, dst, send_sem, recv_sem, device):
    copy = pltpu.make_async_remote_copy(
        src_ref=src, dst_ref=dst, send_sem=send_sem, recv_sem=recv_sem, device_id=device, device_id_type=MESH
    )
    copy.start()
    return copy


def pack_rows(tile_of, out, slots, peers):
    rows = out.shape[1] // slots
    group = max(1, 16 // rows)
    for first in range(0, slots, group):
        tiles = [tile_of(first + k) for k in range(group)]
        for p in range(peers):
            part = [t[p * rows:(p + 1) * rows] for t in tiles]
            part = part[0] if group == 1 else jnp.concatenate(part, axis=0)
            out[p, first * rows:(first + group) * rows, :] = part.astype(out.dtype)


def halves(value):
    high = value.astype(jnp.bfloat16)
    return high, (value - high.astype(jnp.float32)).astype(jnp.bfloat16)


def dot(a, b, contract):
    return lax.dot_general(a, b, (((1,), (contract,)), ((), ())), preferred_element_type=jnp.float32)


def product(value, high, low, contract):
    n = value.shape[0]
    top, bottom = halves(value)
    both = dot(jnp.concatenate([top, bottom], axis=0), high, contract)
    return both[:n] + both[n:] + dot(top, low, contract)


def describe(joined, named, counts, lanes):
    at = lax.broadcasted_iota(jnp.int32, (joined.shape[0], lanes), 1)
    cap = joined.shape[1]
    out = jnp.where(at == 2 * cap, counts, 0)
    for k in range(cap):
        out = jnp.where(at == k, joined[:, k:k + 1], out)
        out = jnp.where(at == cap + k, named[:, k:k + 1], out)
    return out


def spread_kernel(users, items, y_hbm, conf_hbm, held_hbm, ti_ref, tu_ref, tc_ref, hu_ref, hi_ref, hc_ref,
                  y_out, c_out, h_out, mu_out, mi_out, y_ref, conf_ref, held_ref, y_send, c_send, h_send, mu_send, mi_send,
                  z_s, z_r, xy_s, xy_r, sib_s, sib_r, own_s, own_r,
                  c_s, c_r, h_s, h_r, mu_s, mu_r, mi_s, mi_r, local):
    zs = users // 2
    i, u, z, c = place(users, items)
    sibling = (2 * z + 1 - c, i)
    quarter = y_send.shape[2]
    user_peers = [lax.rem(u + k, users) for k in range(1, users)]
    item_peers = [lax.rem(i + e, items) for e in range(1, items)]
    neighbours = [(p, i) for p in user_peers] + [(u, p) for p in item_peers]
    loads = [
        pltpu.make_async_copy(y_hbm, y_ref, local.at[5]),
        pltpu.make_async_copy(held_hbm, held_ref, local.at[6]),
        pltpu.make_async_copy(conf_hbm, conf_ref, local.at[7]),
    ]
    for load in loads:
        load.start()
    greet(neighbours)
    mu_send[...] = jnp.zeros_like(mu_send)
    mi_send[...] = jnp.zeros_like(mi_send)
    mu_send[0:users, :] = describe(ti_ref[...], tu_ref[...], tc_ref[...], mu_send.shape[1])
    mi_send[0:items, :] = describe(hu_ref[...], hi_ref[...], hc_ref[...], mi_send.shape[1])
    loads[0].wait()
    for q in range(items):
        top, bottom = halves(y_ref[q * quarter:(q + 1) * quarter, :])
        y_send[q, 0] = top
        y_send[q, 1] = bottom
    await_greetings(neighbours)

    pending = []
    crossing = []
    for d in range(1, zs):
        peer = 2 * lax.rem(z + d, zs) + c
        crossing.append(send(y_send.at[i], y_out.at[u, i], z_s.at[d], z_r.at[d], (peer, i)))
    pending.append(send(y_send, y_out.at[u], own_s, own_r, sibling))
    keep = [pltpu.make_async_copy(y_send, y_out.at[u], local.at[0])]
    keep[0].start()

    held_slots = held_ref.shape[0]
    loads[1].wait()
    pack_rows(lambda s: held_ref[s].astype(jnp.float32), h_send, held_slots, items)
    for e, p in enumerate(item_peers):
        pending.append(send(h_send.at[p], h_out.at[i], h_s.at[e], h_r.at[e], (u, p)))
        pending.append(send(mi_send, mi_out.at[i], mi_s.at[e], mi_r.at[e], (u, p)))
    for k, p in enumerate(user_peers):
        pending.append(send(mu_send, mu_out.at[u], mu_s.at[k], mu_r.at[k], (p, i)))
    slots = conf_ref.shape[0]
    loads[2].wait()
    pack_rows(lambda s: conf_ref[s].astype(jnp.float32).T, c_send, slots, users)
    keep.append(pltpu.make_async_copy(c_send.at[u], c_out.at[u], local.at[1]))
    keep.append(pltpu.make_async_copy(h_send.at[i], h_out.at[i], local.at[2]))
    keep.append(pltpu.make_async_copy(mu_send, mu_out.at[u], local.at[3]))
    keep.append(pltpu.make_async_copy(mi_send, mi_out.at[i], local.at[4]))
    for copy in keep[1:]:
        copy.start()

    across = {}
    for d in range(1, zs):
        crossing[d - 1].wait_recv()
        shard = 2 * lax.rem(z - d + zs, zs) + c
        block = y_out.at[shard, i]
        for e, p in enumerate(item_peers):
            across[d, e] = send(block, block, xy_s.at[d, e], xy_r.at[d, e], (u, p))
        pending.append(send(block, block, sib_s.at[d, items - 1], sib_r.at[d, items - 1], sibling))
    for k, p in enumerate(user_peers):
        pending.append(send(c_send.at[p], c_out.at[u], c_s.at[k], c_r.at[k], (p, i)))
    for d in range(1, zs):
        shard = 2 * lax.rem(z - d + zs, zs) + c
        for e in range(items - 1):
            across[d, e].wait_recv()
            block = y_out.at[shard, lax.rem(i - e - 1 + items, items)]
            pending.append(send(block, block, sib_s.at[d, e], sib_r.at[d, e], sibling))
    for copy in crossing + list(across.values()):
        copy.wait_send()
    for copy in pending:
        copy.wait()
    for copy in keep:
        copy.wait()


def padded(rows):
    return -(-rows // 8) * 8


def spread(users, items, factors, conf, held, lists, held_lists):
    rows, rank = factors.shape
    slots, width = conf.shape[0], conf.shape[1]
    held_slots = held.shape[0]
    zs = users // 2
    y_piece = (2, rows // items, rank)
    c_piece = (slots * width // users, width)
    h_piece = (held_slots * width // items, width)
    mu_piece, mi_piece = (padded(users), 128), (padded(items), 128)
    dma = pltpu.SemaphoreType.DMA
    bf16, f32 = jnp.bfloat16, jnp.float32
    return pl.pallas_call(
        functools.partial(spread_kernel, users, items),
        out_shape=[
            jax.ShapeDtypeStruct((users, items) + y_piece, bf16),
            jax.ShapeDtypeStruct((users,) + c_piece, bf16),
            jax.ShapeDtypeStruct((items,) + h_piece, bf16),
            jax.ShapeDtypeStruct((users,) + mu_piece, jnp.int32),
            jax.ShapeDtypeStruct((items,) + mi_piece, jnp.int32),
        ],
        in_specs=[HBM] * 3 + [VMEM] * 6,
        out_specs=[ANY] * 5,
        scratch_shapes=[
            pltpu.VMEM((rows, rank), f32),
            pltpu.VMEM(conf.shape, bf16),
            pltpu.VMEM(held.shape, bf16),
            pltpu.VMEM((items,) + y_piece, bf16),
            pltpu.VMEM((users,) + c_piece, bf16),
            pltpu.VMEM((items,) + h_piece, bf16),
            pltpu.VMEM(mu_piece, jnp.int32),
            pltpu.VMEM(mi_piece, jnp.int32),
            dma((zs,)), dma((zs,)), dma((zs, items)), dma((zs, items)), dma((zs, items)), dma((zs, items)),
            dma, dma, dma((users,)), dma((users,)), dma((items,)), dma((items,)),
            dma((users,)), dma((users,)), dma((items,)), dma((items,)), dma((8,)),
        ],
        compiler_params=pltpu.CompilerParams(
            collective_id=0, has_side_effects=True, vmem_limit_bytes=16 * 2**20
        ),
        name="spread_inputs",
    )(factors, conf, held, *lists, *held_lists)


def place_kernel(item_blocks, user_blocks, mu_ref, mi_ref, c_ref, h_ref, w_ref, right_ref, v_ref, held_right_ref):
    def scatter(lists, tiles, weight, right, per_owner, part):
        blocks, rows, width = weight.shape
        sources, piece = tiles.shape[0], tiles.shape[1]
        owners = blocks // per_owner
        slots = piece // part
        cap = slots // owners
        weight[...] = jnp.ones_like(weight)
        right[...] = jnp.zeros_like(right)

        def source_step(source, carry):
            for owner in range(owners):
                for k in range(cap):
                    @pl.when(k < lists[source, owner, 2 * cap])
                    def _():
                        block = owner * per_owner + lists[source, owner, cap + k]
                        at = pl.ds(pl.multiple_of(lists[source, owner, k] * part, part), part)
                        first = (owner * cap + k) * part
                        tile = tiles[source, first:first + part, :].astype(jnp.float32)
                        weight[block, at, :] += tile
                        right[block, at, :] += tile + 1.0
            return carry

        lax.fori_loop(0, sources, source_step, 0)

    scatter(mu_ref, c_ref, w_ref, right_ref, user_blocks, w_ref.shape[1] // item_blocks)
    scatter(mi_ref, h_ref, v_ref, held_right_ref, item_blocks, h_ref.shape[2] // h_ref.shape[0])


def place_tiles(item_blocks, user_blocks, held_blocks, user_lists, item_lists, tiles, held_tiles):
    users, items, width = tiles.shape[0], held_tiles.shape[0], tiles.shape[2]
    item_side = jax.ShapeDtypeStruct((users * user_blocks, item_blocks * width // users, width), jnp.float32)
    held_side = jax.ShapeDtypeStruct((items * item_blocks, held_blocks * width // items, width), jnp.float32)
    return pl.pallas_call(
        functools.partial(place_kernel, item_blocks, user_blocks),
        out_shape=[item_side, item_side, held_side, held_side],
        in_specs=[SMEM, SMEM, VMEM, VMEM],
        out_specs=[VMEM] * 4,
        compiler_params=pltpu.CompilerParams(vmem_limit_bytes=16 * 2**20),
        name="place_tiles",
    )(user_lists, item_lists, tiles, held_tiles)


def conjugate(chunk_of, weight, right, x, rows, rank, chunks):
    per_chunk = weight.shape[0] // chunks

    def wide(ref, n):
        return jnp.concatenate([ref[n * per_chunk + k] for k in range(per_chunk)], axis=1)

    def sweep(coefficients):
        def step(n, total):
            top, bottom = chunk_of(n)
            return total + product(coefficients(n, top, bottom), top, bottom, 0)

        return lax.fori_loop(0, chunks, step, jnp.zeros((rows, rank), jnp.float32), unroll=2)

    def operator(vector):
        return sweep(lambda n, top, bottom: product(vector, top, bottom, 1) * wide(weight, n)) + RIDGE * vector

    if x is None:
        x = jnp.zeros((rows, rank), jnp.float32)
        residual = sweep(lambda n, top, bottom: wide(right, n))
    else:
        residual = sweep(
            lambda n, top, bottom: wide(right, n) - product(x, top, bottom, 1) * wide(weight, n)
        ) - RIDGE * x
    direction = residual
    norm = jnp.sum(residual * residual, axis=1, keepdims=True)
    for iteration in range(ITERS):
        image = operator(direction)
        alpha = norm / (jnp.sum(direction * image, axis=1, keepdims=True) + EPS)
        x = x + alpha * direction
        if iteration + 1 < ITERS:
            residual = residual - alpha * image
            following = jnp.sum(residual * residual, axis=1, keepdims=True)
            direction = residual + following / (norm + EPS) * direction
            norm = following
    return x


def merge_rows(value):
    if value.shape[-2] % 16:
        return value.astype(jnp.float32).reshape(-1, value.shape[-1]).astype(value.dtype)
    return value.reshape(-1, value.shape[-1])


def solve_kernel(users, items, y_ref, start_ref, w_ref, right_ref, v_ref, held_right_ref,
                 new_ref, fold_ref, x_all, x_own, f_own,
                 z_s, z_r, xy_s, xy_r, sib_s, sib_r, f_s, f_r, local):
    zs = users // 2
    i, u, z, c = place(users, items)
    sibling = (2 * z + 1 - c, i)
    z_peers = [2 * lax.rem(z + d, zs) + c for d in range(1, zs)]
    item_peers = [lax.rem(i + e, items) for e in range(1, items)]
    neighbours = [(p, i) for p in z_peers] + [(u, p) for p in item_peers] + [sibling]
    greet(neighbours)

    _, blocks, part, rank = x_own.shape
    x = conjugate(
        lambda n: (merge_rows(y_ref[n, :, 0]), merge_rows(y_ref[n, :, 1])),
        w_ref, right_ref, start_ref[...], blocks * part, rank, users,
    )
    top, bottom = halves(x)
    x_own[0] = top.astype(jnp.float32).reshape(blocks, part, rank).astype(jnp.bfloat16)
    x_own[1] = bottom.astype(jnp.float32).reshape(blocks, part, rank).astype(jnp.bfloat16)
    await_greetings(neighbours)

    crossing, across, pending = [], {}, []
    own = x_all.at[i, :, :, u]
    for d, p in enumerate(z_peers):
        crossing.append(send(x_own, own, z_s.at[d], z_r.at[d], (p, i)))
    for e, p in enumerate(item_peers):
        across[0, e] = send(x_own, own, xy_s.at[0, e], xy_r.at[0, e], (u, p))
    pending.append(send(x_own, own, sib_s.at[0, items - 1], sib_r.at[0, items - 1], sibling))
    keep = pltpu.make_async_copy(x_own, own, local.at[0])
    keep.start()
    for d in range(1, zs):
        crossing[d - 1].wait_recv()
        block = x_all.at[i, :, :, 2 * lax.rem(z - d + zs, zs) + c]
        for e, p in enumerate(item_peers):
            across[d, e] = send(block, block, xy_s.at[d, e], xy_r.at[d, e], (u, p))
        pending.append(send(block, block, sib_s.at[d, items - 1], sib_r.at[d, items - 1], sibling))
    for d in range(zs):
        shard = 2 * lax.rem(z - d + zs, zs) + c
        for e in range(items - 1):
            across[d, e].wait_recv()
            block = x_all.at[lax.rem(i - e - 1 + items, items), :, :, shard]
            pending.append(send(block, block, sib_s.at[d, e], sib_r.at[d, e], sibling))
    for copy in crossing + list(across.values()):
        copy.wait_send()
    for copy in pending:
        copy.wait()
    keep.wait()

    new_ref[...] = merge_rows(x_all[i, 0]).astype(jnp.float32) + merge_rows(x_all[i, 1]).astype(jnp.float32)
    held_blocks, held_part, _ = f_own.shape
    folded = conjugate(
        lambda n: (merge_rows(x_all[n, 0]), merge_rows(x_all[n, 1])),
        v_ref, held_right_ref, None, held_blocks * held_part, rank, items,
    )
    f_own[...] = folded.reshape(held_blocks, held_part, rank)
    mine = fold_ref.at[:, i]
    copies = [send(f_own, mine, f_s.at[e], f_r.at[e], (u, p)) for e, p in enumerate(item_peers)]
    last = pltpu.make_async_copy(f_own, mine, local.at[1])
    last.start()
    for copy in copies:
        copy.wait()
    last.wait()


def solve(users, items, table, start, item_blocks, held_blocks, width, *weights):
    rank = start.shape[1]
    part, held_part = width // users, width // items
    dma = pltpu.SemaphoreType.DMA
    return pl.pallas_call(
        functools.partial(solve_kernel, users, items),
        out_shape=[
            jax.ShapeDtypeStruct((item_blocks * width, rank), jnp.float32),
            jax.ShapeDtypeStruct((held_blocks, items, held_part, rank), jnp.float32),
        ],
        in_specs=[VMEM] * 6,
        out_specs=[VMEM, VMEM],
        scratch_shapes=[
            pltpu.VMEM((items, 2, item_blocks, users, part, rank), jnp.bfloat16),
            pltpu.VMEM((2, item_blocks, part, rank), jnp.bfloat16),
            pltpu.VMEM((held_blocks, held_part, rank), jnp.float32),
            dma((zs := users // 2,)), dma((zs,)),
        ] + [dma((zs, items))] * 4 + [dma((items,)), dma((items,)), dma((2,))],
        compiler_params=pltpu.CompilerParams(
            collective_id=1, has_side_effects=True, vmem_limit_bytes=48 * 2**20
        ),
        name="solve_and_gather",
    )(table, start, *weights)


def shards(user_factors, item_factors, tile_user, tile_item, tile_count, tile_conf,
           held_user, held_item, held_count, held_conf):
    users, items = lax.axis_size("user"), lax.axis_size("item")
    width = tile_conf.shape[-1]
    rank = user_factors.shape[1]
    user_blocks = user_factors.shape[0] // width
    item_blocks = item_factors.shape[0] // width
    held_blocks = 2
    u = lax.axis_index("user")

    conf = tile_conf.reshape(-1, width, width)
    held = held_conf.reshape(-1, width, width)
    lists = (tile_item[0, 0], tile_user[0, 0], tile_count.reshape(-1, 1))
    held_lists = (held_user[0, 0], held_item[0, 0], held_count.reshape(-1, 1))
    table, tiles, held_tiles, user_lists, item_lists = spread(
        users, items, user_factors, conf, held, lists, held_lists
    )
    weights = place_tiles(item_blocks, user_blocks, held_blocks, user_lists, item_lists, tiles, held_tiles)
    start = lax.dynamic_index_in_dim(
        item_factors.reshape(item_blocks, users, width // users, rank), u, axis=1, keepdims=False
    ).reshape(-1, rank)
    new_items, folded = solve(users, items, table, start, item_blocks, held_blocks, width, *weights)
    return new_items, folded.reshape(-1, rank)


def solution(mesh):
    in_specs = (
        P("user", None),
        P("item", None),
        P("item", "user", None, None),
        P("item", "user", None, None),
        P("item", "user", None),
        P("item", "user", None, None, None, None),
        P("user", "item", None, None),
        P("user", "item", None, None),
        P("user", "item", None),
        P("user", "item", None, None, None, None),
    )
    out_specs = (P("item", None), P("user", None))
    return jax.shard_map(shards, mesh=mesh, in_specs=in_specs, out_specs=out_specs, check_vma=False)
```

```python
import functools

import jax
import jax.numpy as jnp
from jax import lax
from jax.experimental import pallas as pl
from jax.experimental.pallas import tpu as pltpu
from jax.sharding import PartitionSpec as P

ITERS = 2
RIDGE = 1.0
EPS = 1e-6
MESH = pl.DeviceIdType.MESH
ANY = pl.BlockSpec(memory_space=pl.ANY)
VMEM = pl.BlockSpec(memory_space=pltpu.VMEM)
HBM = pl.BlockSpec(memory_space=pltpu.HBM)
SMEM = pl.BlockSpec(memory_space=pltpu.SMEM)


def place(users, items):
    u = lax.axis_index("user")
    return lax.axis_index("item"), u, u // 2, lax.rem(u, 2)


def greet(devices):
    for device in devices:
        pl.semaphore_signal(pltpu.get_barrier_semaphore(), inc=1, device_id=device, device_id_type=MESH)


def await_greetings(devices):
    pl.semaphore_wait(pltpu.get_barrier_semaphore(), len(devices))


def send(src, dst, send_sem, recv_sem, device):
    copy = pltpu.make_async_remote_copy(
        src_ref=src, dst_ref=dst, send_sem=send_sem, recv_sem=recv_sem, device_id=device, device_id_type=MESH
    )
    copy.start()
    return copy


def pack_rows(tile_of, out, slots, peers):
    rows = out.shape[1] // slots
    group = max(1, 16 // rows)
    for first in range(0, slots, group):
        tiles = [tile_of(first + k) for k in range(group)]
        for p in range(peers):
            part = [t[p * rows:(p + 1) * rows] for t in tiles]
            part = part[0] if group == 1 else jnp.concatenate(part, axis=0)
            out[p, first * rows:(first + group) * rows, :] = part.astype(out.dtype)


def halves(value):
    high = value.astype(jnp.bfloat16)
    return high, (value - high.astype(jnp.float32)).astype(jnp.bfloat16)


def dot(a, b, contract):
    return lax.dot_general(a, b, (((1,), (contract,)), ((), ())), preferred_element_type=jnp.float32)


def product(value, high, low, contract):
    n = value.shape[0]
    top, bottom = halves(value)
    both = dot(jnp.concatenate([top, bottom], axis=0), high, contract)
    return both[:n] + both[n:] + dot(top, low, contract)


def describe(out, joined, named, counts):
    cap, owners = joined.shape
    out[...] = jnp.zeros_like(out)
    out[0:cap, 0:owners] = joined[...]
    out[cap:2 * cap, 0:owners] = named[...]
    out[2 * cap:2 * cap + 1, 0:owners] = counts[...]


def exchange(items, u, i, d, block, half, sibling, xy_s, xy_r, sib_s, sib_r, sent, pending):
    direct, relays = [], []

    def mirror(q, slot):
        pending.append(send(block(q), block(q), sib_s.at[d, slot], sib_r.at[d, slot], sibling))

    def hop(src, slot, p):
        copy = send(src, src, xy_s.at[d, slot], xy_r.at[d, slot], (u, p))
        sent.append(copy)
        return copy

    if items != 4:
        def first(src):
            for e in range(1, items):
                copy = send(src, block(i), xy_s.at[d, e], xy_r.at[d, e], (u, lax.rem(i + e, items)))
                direct.append(copy)
                sent.append(copy)
            pending.append(send(src, block(i), sib_s.at[d, 0], sib_r.at[d, 0], sibling))

        def second():
            return None

        def third():
            for e in range(1, items):
                direct[e - 1].wait_recv()
                mirror(lax.rem(i - e + items, items), e)

        return first, second, third

    flip = 1 - 2 * lax.rem(i, 2)
    beside, behind = i + flip, lax.rem(i + 2, 4)
    opposite = behind + flip

    def first(src):
        for slot, p in enumerate((beside, behind)):
            copy = send(src, block(i), xy_s.at[d, slot], xy_r.at[d, slot], (u, p))
            direct.append(copy)
            sent.append(copy)
        pending.append(send(src, block(i), sib_s.at[d, 3], sib_r.at[d, 3], sibling))

    def second():
        direct[0].wait_recv()
        relays.append(hop(half(beside, 0), 3, behind))
        mirror(beside, 0)
        direct[1].wait_recv()
        relays.append(hop(half(behind, 1), 2, beside))
        mirror(behind, 1)

    def third():
        for copy in relays:
            copy.wait_recv()
        mirror(opposite, 2)

    return first, second, third


def spread_kernel(users, items, y_hbm, conf_hbm, held_hbm, ti_ref, tu_ref, tc_ref, hu_ref, hi_ref, hc_ref,
                  y_out, c_out, h_out, mu_out, mi_out, y_ref, conf_ref, held_ref, y_send, c_send, h_send, mu_send, mi_send,
                  z_s, z_r, xy_s, xy_r, sib_s, sib_r, own_s, own_r,
                  c_s, c_r, h_s, h_r, mu_s, mu_r, mi_s, mi_r, local):
    zs = users // 2
    i, u, z, c = place(users, items)
    sibling = (2 * z + 1 - c, i)
    quarter = y_send.shape[2]
    user_peers = [lax.rem(u + k, users) for k in range(1, users)]
    item_peers = [lax.rem(i + e, items) for e in range(1, items)]
    neighbours = [(p, i) for p in user_peers] + [(u, p) for p in item_peers]
    loads = [
        pltpu.make_async_copy(y_hbm, y_ref, local.at[5]),
        pltpu.make_async_copy(held_hbm, held_ref, local.at[6]),
        pltpu.make_async_copy(conf_hbm, conf_ref, local.at[7]),
    ]
    for load in loads:
        load.start()
    greet(neighbours)
    describe(mu_send, ti_ref, tu_ref, tc_ref)
    describe(mi_send, hu_ref, hi_ref, hc_ref)
    loads[0].wait()
    for q in range(items):
        top, bottom = halves(y_ref[q * quarter:(q + 1) * quarter, :])
        y_send[q, 0] = top
        y_send[q, 1] = bottom
    await_greetings(neighbours)

    pending = []
    crossing = []
    for d in range(1, zs):
        peer = 2 * lax.rem(z + d, zs) + c
        crossing.append(send(y_send.at[i], y_out.at[u, i], z_s.at[d], z_r.at[d], (peer, i)))
    pending.append(send(y_send, y_out.at[u], own_s, own_r, sibling))
    keep = [pltpu.make_async_copy(y_send, y_out.at[u], local.at[0])]
    keep[0].start()

    held_slots = held_ref.shape[0]
    loads[1].wait()
    pack_rows(lambda s: held_ref[s].astype(jnp.float32), h_send, held_slots, items)
    for e, p in enumerate(item_peers):
        pending.append(send(h_send.at[p], h_out.at[i], h_s.at[e], h_r.at[e], (u, p)))
        pending.append(send(mi_send, mi_out.at[i], mi_s.at[e], mi_r.at[e], (u, p)))
    for k, p in enumerate(user_peers):
        pending.append(send(mu_send, mu_out.at[u], mu_s.at[k], mu_r.at[k], (p, i)))
    slots = conf_ref.shape[0]
    loads[2].wait()
    pack_rows(lambda s: conf_ref[s].astype(jnp.float32).T, c_send, slots, users)
    keep.append(pltpu.make_async_copy(c_send.at[u], c_out.at[u], local.at[1]))
    keep.append(pltpu.make_async_copy(h_send.at[i], h_out.at[i], local.at[2]))
    keep.append(pltpu.make_async_copy(mu_send, mu_out.at[u], local.at[3]))
    keep.append(pltpu.make_async_copy(mi_send, mi_out.at[i], local.at[4]))
    for copy in keep[1:]:
        copy.start()

    sent, stages = [], []
    for d in range(1, zs):
        shard = 2 * lax.rem(z - d + zs, zs) + c
        stages.append(exchange(
            items, u, i, d, lambda q, n=shard: y_out.at[n, q], lambda q, h, n=shard: y_out.at[n, q, h],
            sibling, xy_s, xy_r, sib_s, sib_r, sent, pending,
        ))
    for d in range(1, zs):
        crossing[d - 1].wait_recv()
        stages[d - 1][0](y_out.at[2 * lax.rem(z - d + zs, zs) + c, i])
    for k, p in enumerate(user_peers):
        pending.append(send(c_send.at[p], c_out.at[u], c_s.at[k], c_r.at[k], (p, i)))
    for number in (1, 2):
        for stage in stages:
            stage[number]()
    for copy in crossing + sent:
        copy.wait_send()
    for copy in pending:
        copy.wait()
    for copy in keep:
        copy.wait()


def spread(users, items, factors, conf, held, lists, held_lists):
    rows, rank = factors.shape
    slots, width = conf.shape[0], conf.shape[1]
    held_slots = held.shape[0]
    zs = users // 2
    y_piece = (2, rows // items, rank)
    c_piece = (slots * width // users, width)
    h_piece = (held_slots * width // items, width)
    mu_piece = mi_piece = (8, 128)
    dma = pltpu.SemaphoreType.DMA
    bf16, f32 = jnp.bfloat16, jnp.float32
    return pl.pallas_call(
        functools.partial(spread_kernel, users, items),
        out_shape=[
            jax.ShapeDtypeStruct((users, items) + y_piece, bf16),
            jax.ShapeDtypeStruct((users,) + c_piece, bf16),
            jax.ShapeDtypeStruct((items,) + h_piece, bf16),
            jax.ShapeDtypeStruct((users,) + mu_piece, jnp.int32),
            jax.ShapeDtypeStruct((items,) + mi_piece, jnp.int32),
        ],
        in_specs=[HBM] * 3 + [VMEM] * 6,
        out_specs=[ANY] * 5,
        scratch_shapes=[
            pltpu.VMEM((rows, rank), f32),
            pltpu.VMEM(conf.shape, bf16),
            pltpu.VMEM(held.shape, bf16),
            pltpu.VMEM((items,) + y_piece, bf16),
            pltpu.VMEM((users,) + c_piece, bf16),
            pltpu.VMEM((items,) + h_piece, bf16),
            pltpu.VMEM(mu_piece, jnp.int32),
            pltpu.VMEM(mi_piece, jnp.int32),
            dma((zs,)), dma((zs,)), dma((zs, items)), dma((zs, items)), dma((zs, items)), dma((zs, items)),
            dma, dma, dma((users,)), dma((users,)), dma((items,)), dma((items,)),
            dma((users,)), dma((users,)), dma((items,)), dma((items,)), dma((8,)),
        ],
        compiler_params=pltpu.CompilerParams(
            collective_id=0, has_side_effects=True, vmem_limit_bytes=60 * 2**20
        ),
        name="spread_inputs",
    )(factors, conf, held, *lists, *held_lists)


def place_kernel(item_blocks, user_blocks, mu_ref, mi_ref, c_ref, h_ref, w_ref, right_ref, v_ref, held_right_ref):
    def scatter(lists, tiles, weight, right, per_owner, part):
        blocks, rows, width = weight.shape
        sources, piece = tiles.shape[0], tiles.shape[1]
        owners = blocks // per_owner
        slots = piece // part
        cap = slots // owners
        weight[...] = jnp.ones_like(weight)
        right[...] = jnp.zeros_like(right)

        def source_step(source, carry):
            for owner in range(owners):
                for k in range(cap):
                    @pl.when(k < lists[source, 2 * cap, owner])
                    def _():
                        block = owner * per_owner + lists[source, cap + k, owner]
                        at = pl.ds(pl.multiple_of(lists[source, k, owner] * part, part), part)
                        first = (owner * cap + k) * part
                        tile = tiles[source, first:first + part, :].astype(jnp.float32)
                        weight[block, at, :] += tile
                        right[block, at, :] += tile + 1.0
            return carry

        lax.fori_loop(0, sources, source_step, 0)

    scatter(mu_ref, c_ref, w_ref, right_ref, user_blocks, w_ref.shape[1] // item_blocks)
    scatter(mi_ref, h_ref, v_ref, held_right_ref, item_blocks, h_ref.shape[2] // h_ref.shape[0])


def place_tiles(item_blocks, user_blocks, held_blocks, user_lists, item_lists, tiles, held_tiles):
    users, items, width = tiles.shape[0], held_tiles.shape[0], tiles.shape[2]
    item_side = jax.ShapeDtypeStruct((users * user_blocks, item_blocks * width // users, width), jnp.float32)
    held_side = jax.ShapeDtypeStruct((items * item_blocks, held_blocks * width // items, width), jnp.float32)
    return pl.pallas_call(
        functools.partial(place_kernel, item_blocks, user_blocks),
        out_shape=[item_side, item_side, held_side, held_side],
        in_specs=[SMEM, SMEM, VMEM, VMEM],
        out_specs=[VMEM] * 4,
        compiler_params=pltpu.CompilerParams(vmem_limit_bytes=60 * 2**20),
        name="place_tiles",
    )(user_lists, item_lists, tiles, held_tiles)


def conjugate(chunk_of, weight, right, x, rows, rank, chunks):
    per_chunk = weight.shape[0] // chunks

    def wide(ref, n):
        return jnp.concatenate([ref[n * per_chunk + k] for k in range(per_chunk)], axis=1)

    def sweep(coefficients):
        def step(n, total):
            top, bottom = chunk_of(n)
            return total + product(coefficients(n, top, bottom), top, bottom, 0)

        return lax.fori_loop(0, chunks, step, jnp.zeros((rows, rank), jnp.float32), unroll=2)

    def operator(vector):
        return sweep(lambda n, top, bottom: product(vector, top, bottom, 1) * wide(weight, n)) + RIDGE * vector

    if x is None:
        x = jnp.zeros((rows, rank), jnp.float32)
        residual = sweep(lambda n, top, bottom: wide(right, n))
    else:
        residual = sweep(
            lambda n, top, bottom: wide(right, n) - product(x, top, bottom, 1) * wide(weight, n)
        ) - RIDGE * x
    direction = residual
    norm = jnp.sum(residual * residual, axis=1, keepdims=True)
    for iteration in range(ITERS):
        image = operator(direction)
        alpha = norm / (jnp.sum(direction * image, axis=1, keepdims=True) + EPS)
        x = x + alpha * direction
        if iteration + 1 < ITERS:
            residual = residual - alpha * image
            following = jnp.sum(residual * residual, axis=1, keepdims=True)
            direction = residual + following / (norm + EPS) * direction
            norm = following
    return x


def merge_rows(value):
    if value.shape[-2] % 16:
        return value.astype(jnp.float32).reshape(-1, value.shape[-1]).astype(value.dtype)
    return value.reshape(-1, value.shape[-1])


def solve_kernel(users, items, y_ref, start_ref, w_ref, right_ref, v_ref, held_right_ref,
                 new_ref, fold_ref, x_all, x_own, f_own,
                 z_s, z_r, xy_s, xy_r, sib_s, sib_r, f_s, f_r, local):
    zs = users // 2
    i, u, z, c = place(users, items)
    sibling = (2 * z + 1 - c, i)
    z_peers = [2 * lax.rem(z + d, zs) + c for d in range(1, zs)]
    item_peers = [lax.rem(i + e, items) for e in range(1, items)]
    neighbours = [(p, i) for p in z_peers] + [(u, p) for p in item_peers] + [sibling]
    greet(neighbours)

    _, blocks, part, rank = x_own.shape
    x = conjugate(
        lambda n: (merge_rows(y_ref[n, :, 0]), merge_rows(y_ref[n, :, 1])),
        w_ref, right_ref, start_ref[...], blocks * part, rank, users,
    )
    top, bottom = halves(x)
    x_own[0] = top.astype(jnp.float32).reshape(blocks, part, rank).astype(jnp.bfloat16)
    x_own[1] = bottom.astype(jnp.float32).reshape(blocks, part, rank).astype(jnp.bfloat16)
    await_greetings(neighbours)

    crossing, sent, pending, stages = [], [], [], []
    own = x_all.at[i, :, :, u]
    for d, p in enumerate(z_peers):
        crossing.append(send(x_own, own, z_s.at[d], z_r.at[d], (p, i)))
    for d in range(zs):
        shard = 2 * lax.rem(z - d + zs, zs) + c
        stages.append(exchange(
            items, u, i, d, lambda q, n=shard: x_all.at[q, :, :, n], lambda q, h, n=shard: x_all.at[q, h, :, n],
            sibling, xy_s, xy_r, sib_s, sib_r, sent, pending,
        ))
    stages[0][0](x_own)
    keep = pltpu.make_async_copy(x_own, own, local.at[0])
    keep.start()
    for d in range(1, zs):
        crossing[d - 1].wait_recv()
        stages[d][0](x_all.at[i, :, :, 2 * lax.rem(z - d + zs, zs) + c])
    for number in (1, 2):
        for stage in stages:
            stage[number]()
    for copy in crossing + sent:
        copy.wait_send()
    for copy in pending:
        copy.wait()
    keep.wait()

    new_ref[...] = merge_rows(x_all[i, 0]).astype(jnp.float32) + merge_rows(x_all[i, 1]).astype(jnp.float32)
    held_blocks, held_part, _ = f_own.shape
    folded = conjugate(
        lambda n: (merge_rows(x_all[n, 0]), merge_rows(x_all[n, 1])),
        v_ref, held_right_ref, None, held_blocks * held_part, rank, items,
    )
    f_own[...] = folded.reshape(held_blocks, held_part, rank)
    mine = fold_ref.at[:, i]
    copies = [send(f_own, mine, f_s.at[e], f_r.at[e], (u, p)) for e, p in enumerate(item_peers)]
    last = pltpu.make_async_copy(f_own, mine, local.at[1])
    last.start()
    for copy in copies:
        copy.wait()
    last.wait()


def solve(users, items, table, start, item_blocks, held_blocks, width, *weights):
    rank = start.shape[1]
    part, held_part = width // users, width // items
    dma = pltpu.SemaphoreType.DMA
    return pl.pallas_call(
        functools.partial(solve_kernel, users, items),
        out_shape=[
            jax.ShapeDtypeStruct((item_blocks * width, rank), jnp.float32),
            jax.ShapeDtypeStruct((held_blocks, items, held_part, rank), jnp.float32),
        ],
        in_specs=[VMEM] * 6,
        out_specs=[VMEM, VMEM],
        scratch_shapes=[
            pltpu.VMEM((items, 2, item_blocks, users, part, rank), jnp.bfloat16),
            pltpu.VMEM((2, item_blocks, part, rank), jnp.bfloat16),
            pltpu.VMEM((held_blocks, held_part, rank), jnp.float32),
            dma((zs := users // 2,)), dma((zs,)),
        ] + [dma((zs, items))] * 4 + [dma((items,)), dma((items,)), dma((2,))],
        compiler_params=pltpu.CompilerParams(
            collective_id=1, has_side_effects=True, vmem_limit_bytes=60 * 2**20
        ),
        name="solve_and_gather",
    )(table, start, *weights)


def shards(user_factors, item_factors, tile_user, tile_item, tile_count, tile_conf,
           held_user, held_item, held_count, held_conf):
    users, items = lax.axis_size("user"), lax.axis_size("item")
    width = tile_conf.shape[-1]
    rank = user_factors.shape[1]
    user_blocks = user_factors.shape[0] // width
    item_blocks = item_factors.shape[0] // width
    held_blocks = 2
    u = lax.axis_index("user")

    conf = tile_conf.reshape(-1, width, width)
    held = held_conf.reshape(-1, width, width)
    lists = (tile_item[0, 0].T, tile_user[0, 0].T, tile_count[0])
    held_lists = (held_user[0, 0].T, held_item[0, 0].T, held_count[0])
    table, tiles, held_tiles, user_lists, item_lists = spread(
        users, items, user_factors, conf, held, lists, held_lists
    )
    weights = place_tiles(item_blocks, user_blocks, held_blocks, user_lists, item_lists, tiles, held_tiles)
    start = lax.dynamic_index_in_dim(
        item_factors.reshape(item_blocks, users, width // users, rank), u, axis=1, keepdims=False
    ).reshape(-1, rank)
    new_items, folded = solve(users, items, table, start, item_blocks, held_blocks, width, *weights)
    return new_items, folded.reshape(-1, rank)


def solution(mesh):
    in_specs = (
        P("user", None),
        P("item", None),
        P("item", "user", None, None),
        P("item", "user", None, None),
        P("item", "user", None),
        P("item", "user", None, None, None, None),
        P("user", "item", None, None),
        P("user", "item", None, None),
        P("user", "item", None),
        P("user", "item", None, None, None, None),
    )
    out_specs = (P("item", None), P("user", None))
    return jax.shard_map(shards, mesh=mesh, in_specs=in_specs, out_specs=out_specs, check_vma=False)
```

```python
import functools

import jax
import jax.numpy as jnp
from jax import lax
from jax.experimental import pallas as pl
from jax.experimental.pallas import tpu as pltpu
from jax.sharding import PartitionSpec as P

ITERS = 2
RIDGE = 1.0
EPS = 1e-6
MESH = pl.DeviceIdType.MESH
ANY = pl.BlockSpec(memory_space=pl.ANY)
VMEM = pl.BlockSpec(memory_space=pltpu.VMEM)
HBM = pl.BlockSpec(memory_space=pltpu.HBM)
SMEM = pl.BlockSpec(memory_space=pltpu.SMEM)


def place(users, items):
    u = lax.axis_index("user")
    return lax.axis_index("item"), u, u // 2, lax.rem(u, 2)


def greet(devices):
    for device in devices:
        pl.semaphore_signal(pltpu.get_barrier_semaphore(), inc=1, device_id=device, device_id_type=MESH)


def await_greetings(devices):
    pl.semaphore_wait(pltpu.get_barrier_semaphore(), len(devices))


def send(src, dst, send_sem, recv_sem, device):
    copy = pltpu.make_async_remote_copy(
        src_ref=src, dst_ref=dst, send_sem=send_sem, recv_sem=recv_sem, device_id=device, device_id_type=MESH
    )
    copy.start()
    return copy


def pack_rows(tile_of, out, slots, peers):
    rows = out.shape[1] // slots
    group = max(1, 16 // rows)
    for first in range(0, slots, group):
        tiles = [tile_of(first + k) for k in range(group)]
        for p in range(peers):
            part = [t[p * rows:(p + 1) * rows] for t in tiles]
            part = part[0] if group == 1 else jnp.concatenate(part, axis=0)
            out[p, first * rows:(first + group) * rows, :] = part.astype(out.dtype)


def halves(value):
    high = value.astype(jnp.bfloat16)
    return high, (value - high.astype(jnp.float32)).astype(jnp.bfloat16)


def dot(a, b, contract):
    return lax.dot_general(a, b, (((1,), (contract,)), ((), ())), preferred_element_type=jnp.float32)


def product(value, high, low, contract):
    n = value.shape[0]
    top, bottom = halves(value)
    both = dot(jnp.concatenate([top, bottom], axis=0), high, contract)
    return both[:n] + both[n:] + dot(top, low, contract)


def describe(out, joined, named, counts, per_owner):
    cap, owners = joined.shape
    for owner in range(owners):
        for k in range(cap):
            code = jnp.where(k < counts[0, owner], joined[k, owner] * per_owner + named[k, owner], -1)
            s = owner * cap + k
            out[s:s + 1, :] = jnp.full((1, out.shape[1]), code, jnp.int32)


def place_tiles(codes, tiles, weight, right, per_owner):
    blocks, rows, width = weight.shape
    sources, slots = tiles.shape[0], codes.shape[1]
    part = tiles.shape[1] // slots
    cap = slots * per_owner // blocks
    spans = rows // part

    def step(b, carry):
        owner, inner = b // per_owner, lax.rem(b, per_owner)
        sums = [jnp.zeros((part, width), jnp.float32) for _ in range(spans)]
        counts = [jnp.zeros((8, width), jnp.float32) for _ in range(spans)]
        for source in range(sources):
            first = pl.multiple_of(owner * (cap * part), cap * part)
            both = tiles[source, pl.ds(first, cap * part), :].astype(jnp.float32)
            for k in range(cap):
                tile = both[k * part:(k + 1) * part]
                code = codes[source, pl.ds(owner * cap + k, 1), :]
                for n in range(spans):
                    hit = jnp.broadcast_to(code == n * per_owner + inner, (8, width))
                    counts[n] = counts[n] + jnp.where(hit, 1.0, 0.0)
                    whole = jnp.broadcast_to(code == n * per_owner + inner, (part, width))
                    sums[n] = sums[n] + jnp.where(whole, tile, 0.0)
        for n in range(spans):
            weight[b, n * part:(n + 1) * part, :] = sums[n] + 1.0
            right[b, n * part:(n + 1) * part, :] = sums[n] + jnp.concatenate([counts[n]] * (part // 8), axis=0)
        return carry

    lax.fori_loop(0, blocks, step, 0)


def exchange(items, u, i, d, block, half, sibling, xy_s, xy_r, sib_s, sib_r, sent, pending):
    direct, relays = [], []

    def mirror(q, slot):
        pending.append(send(block(q), block(q), sib_s.at[d, slot], sib_r.at[d, slot], sibling))

    def hop(src, slot, p):
        copy = send(src, src, xy_s.at[d, slot], xy_r.at[d, slot], (u, p))
        sent.append(copy)
        return copy

    if items != 4:
        def first(src):
            for e in range(1, items):
                copy = send(src, block(i), xy_s.at[d, e], xy_r.at[d, e], (u, lax.rem(i + e, items)))
                direct.append(copy)
                sent.append(copy)
            pending.append(send(src, block(i), sib_s.at[d, 0], sib_r.at[d, 0], sibling))

        def second():
            return None

        def third():
            for e in range(1, items):
                direct[e - 1].wait_recv()
                mirror(lax.rem(i - e + items, items), e)

        return first, second, third

    flip = 1 - 2 * lax.rem(i, 2)
    beside, behind = i + flip, lax.rem(i + 2, 4)
    opposite = behind + flip

    def first(src):
        for slot, p in enumerate((beside, behind)):
            copy = send(src, block(i), xy_s.at[d, slot], xy_r.at[d, slot], (u, p))
            direct.append(copy)
            sent.append(copy)
        pending.append(send(src, block(i), sib_s.at[d, 3], sib_r.at[d, 3], sibling))

    def second():
        direct[0].wait_recv()
        relays.append(hop(half(beside, 0), 3, behind))
        mirror(beside, 0)
        direct[1].wait_recv()
        relays.append(hop(half(behind, 1), 2, beside))
        mirror(behind, 1)

    def third():
        for copy in relays:
            copy.wait_recv()
        mirror(opposite, 2)

    return first, second, third


def conjugate(chunk_of, weight, right, x, rows, rank, chunks):
    per_chunk = weight.shape[0] // chunks

    def wide(ref, n):
        return jnp.concatenate([ref[n * per_chunk + k] for k in range(per_chunk)], axis=1)

    def sweep(coefficients):
        def step(n, total):
            top, bottom = chunk_of(n)
            return total + product(coefficients(n, top, bottom), top, bottom, 0)

        return lax.fori_loop(0, chunks, step, jnp.zeros((rows, rank), jnp.float32), unroll=2)

    def operator(vector):
        return sweep(lambda n, top, bottom: product(vector, top, bottom, 1) * wide(weight, n)) + RIDGE * vector

    if x is None:
        x = jnp.zeros((rows, rank), jnp.float32)
        residual = sweep(lambda n, top, bottom: wide(right, n))
    else:
        residual = sweep(
            lambda n, top, bottom: wide(right, n) - product(x, top, bottom, 1) * wide(weight, n)
        ) - RIDGE * x
    direction = residual
    norm = jnp.sum(residual * residual, axis=1, keepdims=True)
    for iteration in range(ITERS):
        image = operator(direction)
        alpha = norm / (jnp.sum(direction * image, axis=1, keepdims=True) + EPS)
        x = x + alpha * direction
        if iteration + 1 < ITERS:
            residual = residual - alpha * image
            following = jnp.sum(residual * residual, axis=1, keepdims=True)
            direction = residual + following / (norm + EPS) * direction
            norm = following
    return x


def merge_rows(value):
    if value.shape[-2] % 16:
        return value.astype(jnp.float32).reshape(-1, value.shape[-1]).astype(value.dtype)
    return value.reshape(-1, value.shape[-1])


def sweep_kernel(users, items, y_hbm, conf_hbm, held_hbm, start_hbm, ti_ref, tu_ref, tc_ref, hu_ref, hi_ref, hc_ref,
                 new_ref, fold_ref,
                 y_out, c_out, h_out, mu_out, mi_out, y_ref, conf_ref, held_ref, start_ref,
                 y_send, c_send, h_send, mu_send, mi_send, w_ref, right_ref, v_ref, held_right_ref, x_all, x_own, f_own,
                 z_s, z_r, xy_s, xy_r, sib_s, sib_r, own_s, own_r, c_s, c_r, h_s, h_r, mu_s, mu_r, mi_s, mi_r,
                 xz_s, xz_r, xxy_s, xxy_r, xsib_s, xsib_r, f_s, f_r, local):
    zs = users // 2
    i, u, z, c = place(users, items)
    sibling = (2 * z + 1 - c, i)
    quarter = y_send.shape[2]
    user_peers = [lax.rem(u + k, users) for k in range(1, users)]
    item_peers = [lax.rem(i + e, items) for e in range(1, items)]
    neighbours = [(p, i) for p in user_peers] + [(u, p) for p in item_peers]
    loads = [
        pltpu.make_async_copy(y_hbm, y_ref, local.at[5]),
        pltpu.make_async_copy(held_hbm, held_ref, local.at[6]),
        pltpu.make_async_copy(conf_hbm, conf_ref, local.at[7]),
        pltpu.make_async_copy(start_hbm.at[:, u], start_ref, local.at[8]),
    ]
    for load in loads:
        load.start()
    greet(neighbours)
    describe(mu_send, ti_ref, tu_ref, tc_ref, w_ref.shape[0] // users)
    describe(mi_send, hu_ref, hi_ref, hc_ref, v_ref.shape[0] // items)
    loads[0].wait()
    for q in range(items):
        top, bottom = halves(y_ref[q * quarter:(q + 1) * quarter, :])
        y_send[q, 0] = top
        y_send[q, 1] = bottom
    await_greetings(neighbours)

    pending, tiled = [], []
    crossing = []
    for d in range(1, zs):
        peer = 2 * lax.rem(z + d, zs) + c
        crossing.append(send(y_send.at[i], y_out.at[u, i], z_s.at[d], z_r.at[d], (peer, i)))
    pending.append(send(y_send, y_out.at[u], own_s, own_r, sibling))
    keep = [pltpu.make_async_copy(y_send, y_out.at[u], local.at[0])]
    keep[0].start()

    held_slots = held_ref.shape[0]
    loads[1].wait()
    pack_rows(lambda s: held_ref[s].astype(jnp.float32), h_send, held_slots, items)
    for e, p in enumerate(item_peers):
        tiled.append(send(h_send.at[p], h_out.at[i], h_s.at[e], h_r.at[e], (u, p)))
        tiled.append(send(mi_send, mi_out.at[i], mi_s.at[e], mi_r.at[e], (u, p)))
    for k, p in enumerate(user_peers):
        tiled.append(send(mu_send, mu_out.at[u], mu_s.at[k], mu_r.at[k], (p, i)))
    slots = conf_ref.shape[0]
    loads[2].wait()
    pack_rows(lambda s: conf_ref[s].astype(jnp.float32).T, c_send, slots, users)
    for k, p in enumerate(user_peers):
        tiled.append(send(c_send.at[p], c_out.at[u], c_s.at[k], c_r.at[k], (p, i)))
    keep.append(pltpu.make_async_copy(c_send.at[u], c_out.at[u], local.at[1]))
    keep.append(pltpu.make_async_copy(h_send.at[i], h_out.at[i], local.at[2]))
    keep.append(pltpu.make_async_copy(mu_send, mu_out.at[u], local.at[3]))
    keep.append(pltpu.make_async_copy(mi_send, mi_out.at[i], local.at[4]))
    for copy in keep[1:]:
        copy.start()

    sent, stages = [], []
    for d in range(1, zs):
        shard = 2 * lax.rem(z - d + zs, zs) + c
        stages.append(exchange(
            items, u, i, d, lambda q, n=shard: y_out.at[n, q], lambda q, h, n=shard: y_out.at[n, q, h],
            sibling, xy_s, xy_r, sib_s, sib_r, sent, pending,
        ))
    for d in range(1, zs):
        crossing[d - 1].wait_recv()
        stages[d - 1][0](y_out.at[2 * lax.rem(z - d + zs, zs) + c, i])
    for stage in stages:
        stage[1]()
    for copy in tiled:
        copy.wait()
    for copy in keep:
        copy.wait()
    loads[3].wait()
    place_tiles(mu_out, c_out, w_ref, right_ref, w_ref.shape[0] // users)
    place_tiles(mi_out, h_out, v_ref, held_right_ref, v_ref.shape[0] // items)
    for stage in stages:
        stage[2]()
    for copy in crossing + sent:
        copy.wait_send()
    for copy in pending:
        copy.wait()

    _, blocks, part, rank = x_own.shape
    x = conjugate(
        lambda n: (merge_rows(y_out[n, :, 0]), merge_rows(y_out[n, :, 1])),
        w_ref, right_ref, start_ref[...].reshape(blocks * part, rank), blocks * part, rank, users,
    )
    top, bottom = halves(x)
    x_own[0] = top.astype(jnp.float32).reshape(blocks, part, rank).astype(jnp.bfloat16)
    x_own[1] = bottom.astype(jnp.float32).reshape(blocks, part, rank).astype(jnp.bfloat16)
    z_peers = [2 * lax.rem(z + d, zs) + c for d in range(1, zs)]
    crossing, sent, pending, stages = [], [], [], []
    own = x_all.at[i, :, :, u]
    for d, p in enumerate(z_peers):
        crossing.append(send(x_own, own, xz_s.at[d], xz_r.at[d], (p, i)))
    for d in range(zs):
        shard = 2 * lax.rem(z - d + zs, zs) + c
        stages.append(exchange(
            items, u, i, d, lambda q, n=shard: x_all.at[q, :, :, n], lambda q, h, n=shard: x_all.at[q, h, :, n],
            sibling, xxy_s, xxy_r, xsib_s, xsib_r, sent, pending,
        ))
    stages[0][0](x_own)
    keep = pltpu.make_async_copy(x_own, own, local.at[9])
    keep.start()
    for d in range(1, zs):
        crossing[d - 1].wait_recv()
        stages[d][0](x_all.at[i, :, :, 2 * lax.rem(z - d + zs, zs) + c])
    for number in (1, 2):
        for stage in stages:
            stage[number]()
    for copy in crossing + sent:
        copy.wait_send()
    for copy in pending:
        copy.wait()
    keep.wait()

    new_ref[...] = merge_rows(x_all[i, 0]).astype(jnp.float32) + merge_rows(x_all[i, 1]).astype(jnp.float32)
    held_blocks, held_part, _ = f_own.shape
    folded = conjugate(
        lambda n: (merge_rows(x_all[n, 0]), merge_rows(x_all[n, 1])),
        v_ref, held_right_ref, None, held_blocks * held_part, rank, items,
    )
    f_own[...] = folded.reshape(held_blocks, held_part, rank)
    mine = fold_ref.at[:, i]
    copies = [send(f_own, mine, f_s.at[e], f_r.at[e], (u, p)) for e, p in enumerate(item_peers)]
    last = pltpu.make_async_copy(f_own, mine, local.at[10])
    last.start()
    for copy in copies:
        copy.wait()
    last.wait()


def sweep(users, items, factors, conf, held, start, lists, held_lists):
    rows, rank = factors.shape
    slots, width = conf.shape[0], conf.shape[1]
    held_slots = held.shape[0]
    item_blocks, _, part, _ = start.shape
    user_blocks, held_blocks, held_part = rows // width, 2, width // items
    zs = users // 2
    y_piece = (2, rows // items, rank)
    c_piece, h_piece = (slots * part, width), (held_slots * held_part, width)
    bf16, f32, i32 = jnp.bfloat16, jnp.float32, jnp.int32
    item_side = (users * user_blocks, item_blocks * part, width)
    held_side = (items * item_blocks, held_blocks * held_part, width)
    dma = pltpu.SemaphoreType.DMA
    rounds = [dma((zs,)), dma((zs,))] + [dma((zs, items))] * 4
    return pl.pallas_call(
        functools.partial(sweep_kernel, users, items),
        out_shape=[
            jax.ShapeDtypeStruct((item_blocks * width, rank), f32),
            jax.ShapeDtypeStruct((held_blocks, items, held_part, rank), f32),
        ],
        in_specs=[HBM] * 4 + [SMEM] * 6,
        out_specs=[VMEM, VMEM],
        scratch_shapes=[
            pltpu.VMEM((users, items) + y_piece, bf16),
            pltpu.VMEM((users,) + c_piece, bf16),
            pltpu.VMEM((items,) + h_piece, bf16),
            pltpu.VMEM((users, slots, width), i32),
            pltpu.VMEM((items, held_slots, width), i32),
            pltpu.VMEM((rows, rank), f32),
            pltpu.VMEM(conf.shape, bf16),
            pltpu.VMEM(held.shape, bf16),
            pltpu.VMEM((item_blocks, part, rank), f32),
            pltpu.VMEM((items,) + y_piece, bf16),
            pltpu.VMEM((users,) + c_piece, bf16),
            pltpu.VMEM((items,) + h_piece, bf16),
            pltpu.VMEM((slots, width), i32),
            pltpu.VMEM((held_slots, width), i32),
            pltpu.VMEM(item_side, f32),
            pltpu.VMEM(item_side, f32),
            pltpu.VMEM(held_side, f32),
            pltpu.VMEM(held_side, f32),
            pltpu.VMEM((items, 2, item_blocks, users, part, rank), bf16),
            pltpu.VMEM((2, item_blocks, part, rank), bf16),
            pltpu.VMEM((held_blocks, held_part, rank), f32),
        ] + rounds + [dma, dma, dma((users,)), dma((users,)), dma((items,)), dma((items,)),
                      dma((users,)), dma((users,)), dma((items,)), dma((items,))]
        + rounds + [dma((items,)), dma((items,)), dma((11,))],
        compiler_params=pltpu.CompilerParams(
            collective_id=0, has_side_effects=True, vmem_limit_bytes=60 * 2**20
        ),
        name="sweep",
    )(factors, conf, held, start, *lists, *held_lists)


def shards(user_factors, item_factors, tile_user, tile_item, tile_count, tile_conf,
           held_user, held_item, held_count, held_conf):
    users, items = lax.axis_size("user"), lax.axis_size("item")
    width = tile_conf.shape[-1]
    rank = user_factors.shape[1]
    new_items, folded = sweep(
        users, items, user_factors,
        tile_conf.reshape(-1, width, width), held_conf.reshape(-1, width, width),
        item_factors.reshape(item_factors.shape[0] // width, users, width // users, rank),
        (tile_item[0, 0].T, tile_user[0, 0].T, tile_count[0]),
        (held_user[0, 0].T, held_item[0, 0].T, held_count[0]),
    )
    return new_items, folded.reshape(-1, rank)


def solution(mesh):
    in_specs = (
        P("user", None),
        P("item", None),
        P("item", "user", None, None),
        P("item", "user", None, None),
        P("item", "user", None),
        P("item", "user", None, None, None, None),
        P("user", "item", None, None),
        P("user", "item", None, None),
        P("user", "item", None),
        P("user", "item", None, None, None, None),
    )
    out_specs = (P("item", None), P("user", None))
    return jax.shard_map(shards, mesh=mesh, in_specs=in_specs, out_specs=out_specs, check_vma=False)
```

```python
import functools

import jax
import jax.numpy as jnp
from jax import lax
from jax.experimental import pallas as pl
from jax.experimental.pallas import tpu as pltpu
from jax.sharding import PartitionSpec as P

ITERS = 2
RIDGE = 1.0
EPS = 1e-6
MESH = pl.DeviceIdType.MESH
ANY = pl.BlockSpec(memory_space=pl.ANY)
VMEM = pl.BlockSpec(memory_space=pltpu.VMEM)
HBM = pl.BlockSpec(memory_space=pltpu.HBM)
SMEM = pl.BlockSpec(memory_space=pltpu.SMEM)


def place(users, items):
    u = lax.axis_index("user")
    return lax.axis_index("item"), u, u // 2, lax.rem(u, 2)


def greet(devices):
    for device in devices:
        pl.semaphore_signal(pltpu.get_barrier_semaphore(), inc=1, device_id=device, device_id_type=MESH)


def await_greetings(devices):
    pl.semaphore_wait(pltpu.get_barrier_semaphore(), len(devices))


def send(src, dst, send_sem, recv_sem, device):
    copy = pltpu.make_async_remote_copy(
        src_ref=src, dst_ref=dst, send_sem=send_sem, recv_sem=recv_sem, device_id=device, device_id_type=MESH
    )
    copy.start()
    return copy


def pack_rows(tile_of, out, slots, peers):
    rows = out.shape[1] // slots
    group = max(1, 16 // rows)
    for first in range(0, slots, group):
        tiles = [tile_of(first + k) for k in range(group)]
        for p in range(peers):
            part = [t[p * rows:(p + 1) * rows] for t in tiles]
            part = part[0] if group == 1 else jnp.concatenate(part, axis=0)
            out[p, first * rows:(first + group) * rows, :] = part.astype(out.dtype)


def halves(value):
    high = value.astype(jnp.bfloat16)
    return high, (value - high.astype(jnp.float32)).astype(jnp.bfloat16)


def dot(a, b, contract):
    return lax.dot_general(a, b, (((1,), (contract,)), ((), ())), preferred_element_type=jnp.float32)


def product(value, high, low, contract):
    n = value.shape[0]
    top, bottom = halves(value)
    both = dot(jnp.concatenate([top, bottom], axis=0), high, contract)
    return both[:n] + both[n:] + dot(top, low, contract)


def describe(out, joined, named, counts, per_owner):
    cap, owners = joined.shape
    for owner in range(owners):
        for k in range(cap):
            code = jnp.where(k < counts[0, owner], joined[k, owner] * per_owner + named[k, owner], -1)
            s = owner * cap + k
            out[s:s + 1, :] = jnp.full((1, out.shape[1]), code, jnp.int32)


def place_tiles(codes, tiles, weight, right, per_owner):
    blocks, rows, width = weight.shape
    sources, slots = tiles.shape[0], codes.shape[1]
    part = tiles.shape[1] // slots
    cap = slots * per_owner // blocks
    spans = rows // part

    def step(b, carry):
        owner, inner = b // per_owner, lax.rem(b, per_owner)
        sums = [jnp.zeros((part, width), jnp.float32) for _ in range(spans)]
        counts = [jnp.zeros((8, width), jnp.float32) for _ in range(spans)]
        for source in range(sources):
            first = pl.multiple_of(owner * (cap * part), cap * part)
            both = tiles[source, pl.ds(first, cap * part), :].astype(jnp.float32)
            for k in range(cap):
                tile = both[k * part:(k + 1) * part]
                code = codes[source, pl.ds(owner * cap + k, 1), :]
                for n in range(spans):
                    hit = jnp.broadcast_to(code == n * per_owner + inner, (8, width))
                    counts[n] = counts[n] + jnp.where(hit, 1.0, 0.0)
                    whole = jnp.broadcast_to(code == n * per_owner + inner, (part, width))
                    sums[n] = sums[n] + jnp.where(whole, tile, 0.0)
        for n in range(spans):
            weight[b, n * part:(n + 1) * part, :] = sums[n] + 1.0
            right[b, n * part:(n + 1) * part, :] = sums[n] + jnp.concatenate([counts[n]] * (part // 8), axis=0)
        return carry

    lax.fori_loop(0, blocks, step, 0)


def by_distance(z, zs):
    near = jnp.minimum(z, zs - 1 - z)
    order = []
    for k in range(zs - 1):
        beside = z - (k // 2 + 1) if k % 2 == 0 else z + (k // 2 + 1)
        step = k - near + 1
        beyond = jnp.where(2 * z < zs - 1, z + step, z - step)
        order.append(jnp.where(k < 2 * near, beside, beyond))
    return order


def chain(i, z, c, zs, order, own, block, z_s, z_r):
    def to(src, dst, slot, n, place):
        inside = jnp.logical_and(place >= 0, place < zs)
        device = (2 * jnp.clip(place, 0, zs - 1) + c, i)
        return inside, pltpu.make_async_remote_copy(
            src_ref=src, dst_ref=dst, send_sem=z_s.at[slot], recv_sem=z_r.at[n],
            device_id=device, device_id_type=MESH,
        )

    moves = [to(own, block(z), 0, z, z + 1), to(own, block(z), 1, z, z - 1)]
    onward = [to(block(n), block(n), 2 + k, n, jnp.where(n < z, z + 1, z - 1)) for k, n in enumerate(order)]

    def start(move):
        pl.when(move[0])(lambda: move[1].start())

    for move in moves:
        start(move)

    def take(k):
        onward[k][1].wait_recv()
        start(onward[k])

    def close():
        for inside, copy in moves + onward:
            pl.when(inside)(copy.wait_send)

    return take, close


def exchange(items, u, i, d, block, half, sibling, xy_s, xy_r, sib_s, sib_r, sent, pending):
    direct, relays = [], []

    def mirror(q, slot):
        pending.append(send(block(q), block(q), sib_s.at[d, slot], sib_r.at[d, slot], sibling))

    def hop(src, slot, p):
        copy = send(src, src, xy_s.at[d, slot], xy_r.at[d, slot], (u, p))
        sent.append(copy)
        return copy

    if items != 4:
        def first(src):
            for e in range(1, items):
                copy = send(src, block(i), xy_s.at[d, e], xy_r.at[d, e], (u, lax.rem(i + e, items)))
                direct.append(copy)
                sent.append(copy)
            pending.append(send(src, block(i), sib_s.at[d, 0], sib_r.at[d, 0], sibling))

        def second():
            return None

        def third():
            for e in range(1, items):
                direct[e - 1].wait_recv()
                mirror(lax.rem(i - e + items, items), e)

        return first, second, third

    flip = 1 - 2 * lax.rem(i, 2)
    beside, behind = i + flip, lax.rem(i + 2, 4)
    opposite = behind + flip

    def first(src):
        for slot, p in enumerate((beside, behind)):
            copy = send(src, block(i), xy_s.at[d, slot], xy_r.at[d, slot], (u, p))
            direct.append(copy)
            sent.append(copy)
        pending.append(send(src, block(i), sib_s.at[d, 3], sib_r.at[d, 3], sibling))

    def second():
        direct[0].wait_recv()
        relays.append(hop(half(beside, 0), 3, behind))
        mirror(beside, 0)
        direct[1].wait_recv()
        relays.append(hop(half(behind, 1), 2, beside))
        mirror(behind, 1)

    def third():
        for copy in relays:
            copy.wait_recv()
        mirror(opposite, 2)

    return first, second, third


def conjugate(chunk_of, weight, right, x, rows, rank, chunks):
    per_chunk = weight.shape[0] // chunks

    def wide(ref, n):
        return jnp.concatenate([ref[n * per_chunk + k] for k in range(per_chunk)], axis=1)

    def sweep(coefficients):
        def step(n, total):
            top, bottom = chunk_of(n)
            return total + product(coefficients(n, top, bottom), top, bottom, 0)

        return lax.fori_loop(0, chunks, step, jnp.zeros((rows, rank), jnp.float32), unroll=2)

    def operator(vector):
        return sweep(lambda n, top, bottom: product(vector, top, bottom, 1) * wide(weight, n)) + RIDGE * vector

    if x is None:
        x = jnp.zeros((rows, rank), jnp.float32)
        residual = sweep(lambda n, top, bottom: wide(right, n))
    else:
        residual = sweep(
            lambda n, top, bottom: wide(right, n) - product(x, top, bottom, 1) * wide(weight, n)
        ) - RIDGE * x
    direction = residual
    norm = jnp.sum(residual * residual, axis=1, keepdims=True)
    for iteration in range(ITERS):
        image = operator(direction)
        alpha = norm / (jnp.sum(direction * image, axis=1, keepdims=True) + EPS)
        x = x + alpha * direction
        if iteration + 1 < ITERS:
            residual = residual - alpha * image
            following = jnp.sum(residual * residual, axis=1, keepdims=True)
            direction = residual + following / (norm + EPS) * direction
            norm = following
    return x


def merge_rows(value):
    if value.shape[-2] % 16:
        return value.astype(jnp.float32).reshape(-1, value.shape[-1]).astype(value.dtype)
    return value.reshape(-1, value.shape[-1])


def sweep_kernel(users, items, y_hbm, conf_hbm, held_hbm, start_hbm, ti_ref, tu_ref, tc_ref, hu_ref, hi_ref, hc_ref,
                 new_ref, fold_ref,
                 y_out, c_out, h_out, mu_out, mi_out, y_ref, conf_ref, held_ref, start_ref,
                 y_send, c_send, h_send, mu_send, mi_send, w_ref, right_ref, v_ref, held_right_ref, x_all, x_own, f_own,
                 z_s, z_r, xy_s, xy_r, sib_s, sib_r, own_s, own_r, c_s, c_r, h_s, h_r, mu_s, mu_r, mi_s, mi_r,
                 xz_s, xz_r, xxy_s, xxy_r, xsib_s, xsib_r, f_s, f_r, local):
    zs = users // 2
    i, u, z, c = place(users, items)
    sibling = (2 * z + 1 - c, i)
    quarter = y_send.shape[2]
    user_peers = [lax.rem(u + k, users) for k in range(1, users)]
    item_peers = [lax.rem(i + e, items) for e in range(1, items)]
    neighbours = [(p, i) for p in user_peers] + [(u, p) for p in item_peers]
    loads = [
        pltpu.make_async_copy(y_hbm, y_ref, local.at[5]),
        pltpu.make_async_copy(held_hbm, held_ref, local.at[6]),
        pltpu.make_async_copy(conf_hbm, conf_ref, local.at[7]),
        pltpu.make_async_copy(start_hbm.at[:, u], start_ref, local.at[8]),
    ]
    for load in loads:
        load.start()
    greet(neighbours)
    describe(mu_send, ti_ref, tu_ref, tc_ref, w_ref.shape[0] // users)
    describe(mi_send, hu_ref, hi_ref, hc_ref, v_ref.shape[0] // items)
    loads[0].wait()
    for q in range(items):
        top, bottom = halves(y_ref[q * quarter:(q + 1) * quarter, :])
        y_send[q, 0] = top
        y_send[q, 1] = bottom
    await_greetings(neighbours)

    pending, tiled = [], []
    order = by_distance(z, zs)
    take, close = chain(i, z, c, zs, order, y_send.at[i], lambda n: y_out.at[2 * n + c, i], z_s, z_r)
    pending.append(send(y_send, y_out.at[u], own_s, own_r, sibling))
    keep = [pltpu.make_async_copy(y_send, y_out.at[u], local.at[0])]
    keep[0].start()

    held_slots = held_ref.shape[0]
    loads[1].wait()
    pack_rows(lambda s: held_ref[s].astype(jnp.float32), h_send, held_slots, items)
    for e, p in enumerate(item_peers):
        tiled.append(send(h_send.at[p], h_out.at[i], h_s.at[e], h_r.at[e], (u, p)))
        tiled.append(send(mi_send, mi_out.at[i], mi_s.at[e], mi_r.at[e], (u, p)))
    for k, p in enumerate(user_peers):
        tiled.append(send(mu_send, mu_out.at[u], mu_s.at[k], mu_r.at[k], (p, i)))
    slots = conf_ref.shape[0]
    loads[2].wait()
    pack_rows(lambda s: conf_ref[s].astype(jnp.float32).T, c_send, slots, users)
    for k, p in enumerate(user_peers):
        tiled.append(send(c_send.at[p], c_out.at[u], c_s.at[k], c_r.at[k], (p, i)))
    keep.append(pltpu.make_async_copy(c_send.at[u], c_out.at[u], local.at[1]))
    keep.append(pltpu.make_async_copy(h_send.at[i], h_out.at[i], local.at[2]))
    keep.append(pltpu.make_async_copy(mu_send, mu_out.at[u], local.at[3]))
    keep.append(pltpu.make_async_copy(mi_send, mi_out.at[i], local.at[4]))
    for copy in keep[1:]:
        copy.start()

    sent, stages = [], []
    for d, n in enumerate(order):
        shard = 2 * n + c
        stages.append(exchange(
            items, u, i, d, lambda q, n=shard: y_out.at[n, q], lambda q, h, n=shard: y_out.at[n, q, h],
            sibling, xy_s, xy_r, sib_s, sib_r, sent, pending,
        ))
    for d, n in enumerate(order):
        take(d)
        stages[d][0](y_out.at[2 * n + c, i])
    for stage in stages:
        stage[1]()
    for copy in tiled:
        copy.wait()
    for copy in keep:
        copy.wait()
    loads[3].wait()
    place_tiles(mu_out, c_out, w_ref, right_ref, w_ref.shape[0] // users)
    place_tiles(mi_out, h_out, v_ref, held_right_ref, v_ref.shape[0] // items)
    for stage in stages:
        stage[2]()
    close()
    for copy in sent:
        copy.wait_send()
    for copy in pending:
        copy.wait()

    _, blocks, part, rank = x_own.shape
    x = conjugate(
        lambda n: (merge_rows(y_out[n, :, 0]), merge_rows(y_out[n, :, 1])),
        w_ref, right_ref, start_ref[...].reshape(blocks * part, rank), blocks * part, rank, users,
    )
    top, bottom = halves(x)
    x_own[0] = top.astype(jnp.float32).reshape(blocks, part, rank).astype(jnp.bfloat16)
    x_own[1] = bottom.astype(jnp.float32).reshape(blocks, part, rank).astype(jnp.bfloat16)
    sent, pending, stages = [], [], []
    own = x_all.at[i, :, :, u]
    take, close = chain(i, z, c, zs, order, x_own, lambda n: x_all.at[i, :, :, 2 * n + c], xz_s, xz_r)
    for d, n in enumerate([z] + order):
        shard = 2 * n + c
        stages.append(exchange(
            items, u, i, d, lambda q, n=shard: x_all.at[q, :, :, n], lambda q, h, n=shard: x_all.at[q, h, :, n],
            sibling, xxy_s, xxy_r, xsib_s, xsib_r, sent, pending,
        ))
    stages[0][0](x_own)
    keep = pltpu.make_async_copy(x_own, own, local.at[9])
    keep.start()
    for d, n in enumerate(order):
        take(d)
        stages[d + 1][0](x_all.at[i, :, :, 2 * n + c])
    for number in (1, 2):
        for stage in stages:
            stage[number]()
    close()
    for copy in sent:
        copy.wait_send()
    for copy in pending:
        copy.wait()
    keep.wait()

    new_ref[...] = merge_rows(x_all[i, 0]).astype(jnp.float32) + merge_rows(x_all[i, 1]).astype(jnp.float32)
    held_blocks, held_part, _ = f_own.shape
    folded = conjugate(
        lambda n: (merge_rows(x_all[n, 0]), merge_rows(x_all[n, 1])),
        v_ref, held_right_ref, None, held_blocks * held_part, rank, items,
    )
    f_own[...] = folded.reshape(held_blocks, held_part, rank)
    mine = fold_ref.at[:, i]
    copies = [send(f_own, mine, f_s.at[e], f_r.at[e], (u, p)) for e, p in enumerate(item_peers)]
    last = pltpu.make_async_copy(f_own, mine, local.at[10])
    last.start()
    for copy in copies:
        copy.wait()
    last.wait()


def sweep(users, items, factors, conf, held, start, lists, held_lists):
    rows, rank = factors.shape
    slots, width = conf.shape[0], conf.shape[1]
    held_slots = held.shape[0]
    item_blocks, _, part, _ = start.shape
    user_blocks, held_blocks, held_part = rows // width, 2, width // items
    zs = users // 2
    y_piece = (2, rows // items, rank)
    c_piece, h_piece = (slots * part, width), (held_slots * held_part, width)
    bf16, f32, i32 = jnp.bfloat16, jnp.float32, jnp.int32
    item_side = (users * user_blocks, item_blocks * part, width)
    held_side = (items * item_blocks, held_blocks * held_part, width)
    dma = pltpu.SemaphoreType.DMA
    rounds = [dma((zs + 1,)), dma((zs,))] + [dma((zs, items))] * 4
    return pl.pallas_call(
        functools.partial(sweep_kernel, users, items),
        out_shape=[
            jax.ShapeDtypeStruct((item_blocks * width, rank), f32),
            jax.ShapeDtypeStruct((held_blocks, items, held_part, rank), f32),
        ],
        in_specs=[HBM] * 4 + [SMEM] * 6,
        out_specs=[VMEM, VMEM],
        scratch_shapes=[
            pltpu.VMEM((users, items) + y_piece, bf16),
            pltpu.VMEM((users,) + c_piece, bf16),
            pltpu.VMEM((items,) + h_piece, bf16),
            pltpu.VMEM((users, slots, width), i32),
            pltpu.VMEM((items, held_slots, width), i32),
            pltpu.VMEM((rows, rank), f32),
            pltpu.VMEM(conf.shape, bf16),
            pltpu.VMEM(held.shape, bf16),
            pltpu.VMEM((item_blocks, part, rank), f32),
            pltpu.VMEM((items,) + y_piece, bf16),
            pltpu.VMEM((users,) + c_piece, bf16),
            pltpu.VMEM((items,) + h_piece, bf16),
            pltpu.VMEM((slots, width), i32),
            pltpu.VMEM((held_slots, width), i32),
            pltpu.VMEM(item_side, f32),
            pltpu.VMEM(item_side, f32),
            pltpu.VMEM(held_side, f32),
            pltpu.VMEM(held_side, f32),
            pltpu.VMEM((items, 2, item_blocks, users, part, rank), bf16),
            pltpu.VMEM((2, item_blocks, part, rank), bf16),
            pltpu.VMEM((held_blocks, held_part, rank), f32),
        ] + rounds + [dma, dma, dma((users,)), dma((users,)), dma((items,)), dma((items,)),
                      dma((users,)), dma((users,)), dma((items,)), dma((items,))]
        + rounds + [dma((items,)), dma((items,)), dma((11,))],
        compiler_params=pltpu.CompilerParams(
            collective_id=0, has_side_effects=True, vmem_limit_bytes=60 * 2**20
        ),
        name="sweep",
    )(factors, conf, held, start, *lists, *held_lists)


def shards(user_factors, item_factors, tile_user, tile_item, tile_count, tile_conf,
           held_user, held_item, held_count, held_conf):
    users, items = lax.axis_size("user"), lax.axis_size("item")
    width = tile_conf.shape[-1]
    rank = user_factors.shape[1]
    new_items, folded = sweep(
        users, items, user_factors,
        tile_conf.reshape(-1, width, width), held_conf.reshape(-1, width, width),
        item_factors.reshape(item_factors.shape[0] // width, users, width // users, rank),
        (tile_item[0, 0].T, tile_user[0, 0].T, tile_count[0]),
        (held_user[0, 0].T, held_item[0, 0].T, held_count[0]),
    )
    return new_items, folded.reshape(-1, rank)


def solution(mesh):
    in_specs = (
        P("user", None),
        P("item", None),
        P("item", "user", None, None),
        P("item", "user", None, None),
        P("item", "user", None),
        P("item", "user", None, None, None, None),
        P("user", "item", None, None),
        P("user", "item", None, None),
        P("user", "item", None),
        P("user", "item", None, None, None, None),
    )
    out_specs = (P("item", None), P("user", None))
    return jax.shard_map(shards, mesh=mesh, in_specs=in_specs, out_specs=out_specs, check_vma=False)
```

```python
import functools

import jax
import jax.numpy as jnp
from jax import lax
from jax.experimental import pallas as pl
from jax.experimental.pallas import tpu as pltpu
from jax.sharding import PartitionSpec as P

ITERS = 2
RIDGE = 1.0
EPS = 1e-6
MESH = pl.DeviceIdType.MESH
ANY = pl.BlockSpec(memory_space=pl.ANY)
VMEM = pl.BlockSpec(memory_space=pltpu.VMEM)
HBM = pl.BlockSpec(memory_space=pltpu.HBM)
SMEM = pl.BlockSpec(memory_space=pltpu.SMEM)


def place(users, items):
    u = lax.axis_index("user")
    return lax.axis_index("item"), u, u // 2, lax.rem(u, 2)


def greet(devices):
    for device in devices:
        pl.semaphore_signal(pltpu.get_barrier_semaphore(), inc=1, device_id=device, device_id_type=MESH)


def await_greetings(devices):
    pl.semaphore_wait(pltpu.get_barrier_semaphore(), len(devices))


def send(src, dst, send_sem, recv_sem, device):
    copy = pltpu.make_async_remote_copy(
        src_ref=src, dst_ref=dst, send_sem=send_sem, recv_sem=recv_sem, device_id=device, device_id_type=MESH
    )
    copy.start()
    return copy


def pack_rows(tile_of, out, slots, peers):
    rows = out.shape[1] // slots
    group = max(1, 16 // rows)
    for first in range(0, slots, group):
        tiles = [tile_of(first + k) for k in range(group)]
        for p in range(peers):
            part = [t[p * rows:(p + 1) * rows] for t in tiles]
            part = part[0] if group == 1 else jnp.concatenate(part, axis=0)
            out[p, first * rows:(first + group) * rows, :] = part.astype(out.dtype)


def halves(value):
    high = value.astype(jnp.bfloat16)
    return high, (value - high.astype(jnp.float32)).astype(jnp.bfloat16)


def dot(a, b, contract):
    return lax.dot_general(a, b, (((1,), (contract,)), ((), ())), preferred_element_type=jnp.float32)


def product(value, high, low, contract):
    n = value.shape[0]
    top, bottom = halves(value)
    both = dot(jnp.concatenate([top, bottom], axis=0), high, contract)
    return both[:n] + both[n:] + dot(top, low, contract)


def describe(out, joined, named, counts, per_owner):
    cap, owners = joined.shape
    for owner in range(owners):
        for k in range(cap):
            code = jnp.where(k < counts[0, owner], joined[k, owner] * per_owner + named[k, owner], -1)
            s = owner * cap + k
            out[s:s + 1, :] = jnp.full((1, out.shape[1]), code, jnp.int32)


def place_tiles(codes, tiles, weight, right, per_owner):
    blocks, rows, width = weight.shape
    sources, slots = tiles.shape[0], codes.shape[1]
    part = tiles.shape[1] // slots
    cap = slots * per_owner // blocks
    spans = rows // part

    def step(b, carry):
        owner, inner = b // per_owner, lax.rem(b, per_owner)
        sums = [jnp.zeros((part, width), jnp.float32) for _ in range(spans)]
        counts = [jnp.zeros((8, width), jnp.float32) for _ in range(spans)]
        for source in range(sources):
            first = pl.multiple_of(owner * (cap * part), cap * part)
            both = tiles[source, pl.ds(first, cap * part), :].astype(jnp.float32)
            for k in range(cap):
                tile = both[k * part:(k + 1) * part]
                code = codes[source, pl.ds(owner * cap + k, 1), :]
                for n in range(spans):
                    hit = jnp.broadcast_to(code == n * per_owner + inner, (8, width))
                    counts[n] = counts[n] + jnp.where(hit, 1.0, 0.0)
                    whole = jnp.broadcast_to(code == n * per_owner + inner, (part, width))
                    sums[n] = sums[n] + jnp.where(whole, tile, 0.0)
        for n in range(spans):
            weight[b, n * part:(n + 1) * part, :] = sums[n] + 1.0
            right[b, n * part:(n + 1) * part, :] = sums[n] + jnp.concatenate([counts[n]] * (part // 8), axis=0)
        return carry

    lax.fori_loop(0, blocks, step, 0)


def exchange(items, u, i, d, block, half, sibling, xy_s, xy_r, sib_s, sib_r, sent, pending):
    direct, relays = [], []

    def mirror(q, slot):
        pending.append(send(block(q), block(q), sib_s.at[d, slot], sib_r.at[d, slot], sibling))

    def hop(src, slot, p):
        copy = send(src, src, xy_s.at[d, slot], xy_r.at[d, slot], (u, p))
        sent.append(copy)
        return copy

    if items != 4:
        def first(src):
            for e in range(1, items):
                copy = send(src, block(i), xy_s.at[d, e], xy_r.at[d, e], (u, lax.rem(i + e, items)))
                direct.append(copy)
                sent.append(copy)
            pending.append(send(src, block(i), sib_s.at[d, 0], sib_r.at[d, 0], sibling))

        def second():
            return None

        def third():
            for e in range(1, items):
                direct[e - 1].wait_recv()
                mirror(lax.rem(i - e + items, items), e)

        return first, second, third

    flip = 1 - 2 * lax.rem(i, 2)
    beside, behind = i + flip, lax.rem(i + 2, 4)
    opposite = behind + flip

    def first(src):
        for slot, p in enumerate((beside, behind)):
            copy = send(src, block(i), xy_s.at[d, slot], xy_r.at[d, slot], (u, p))
            direct.append(copy)
            sent.append(copy)
        pending.append(send(src, block(i), sib_s.at[d, 3], sib_r.at[d, 3], sibling))

    def second():
        direct[0].wait_recv()
        relays.append(hop(half(beside, 0), 3, behind))
        mirror(beside, 0)
        direct[1].wait_recv()
        relays.append(hop(half(behind, 1), 2, beside))
        mirror(behind, 1)

    def third():
        for copy in relays:
            copy.wait_recv()
        mirror(opposite, 2)

    return first, second, third


def conjugate(chunk_of, weight, right, x, rows, rank, chunks):
    per_chunk = weight.shape[0] // chunks

    def wide(ref, n):
        return jnp.concatenate([ref[n * per_chunk + k] for k in range(per_chunk)], axis=1)

    def sweep(coefficients):
        def step(n, total):
            top, bottom = chunk_of(n)
            return total + product(coefficients(n, top, bottom), top, bottom, 0)

        return lax.fori_loop(0, chunks, step, jnp.zeros((rows, rank), jnp.float32), unroll=4)

    def operator(vector):
        return sweep(lambda n, top, bottom: product(vector, top, bottom, 1) * wide(weight, n)) + RIDGE * vector

    if x is None:
        x = jnp.zeros((rows, rank), jnp.float32)
        residual = sweep(lambda n, top, bottom: wide(right, n))
    else:
        residual = sweep(
            lambda n, top, bottom: wide(right, n) - product(x, top, bottom, 1) * wide(weight, n)
        ) - RIDGE * x
    direction = residual
    norm = jnp.sum(residual * residual, axis=1, keepdims=True)
    for iteration in range(ITERS):
        image = operator(direction)
        alpha = norm / (jnp.sum(direction * image, axis=1, keepdims=True) + EPS)
        x = x + alpha * direction
        if iteration + 1 < ITERS:
            residual = residual - alpha * image
            following = jnp.sum(residual * residual, axis=1, keepdims=True)
            direction = residual + following / (norm + EPS) * direction
            norm = following
    return x


def merge_rows(value):
    if value.shape[-2] % 16:
        return value.astype(jnp.float32).reshape(-1, value.shape[-1]).astype(value.dtype)
    return value.reshape(-1, value.shape[-1])


def sweep_kernel(users, items, y_hbm, conf_hbm, held_hbm, start_hbm, ti_ref, tu_ref, tc_ref, hu_ref, hi_ref, hc_ref,
                 new_ref, fold_ref,
                 y_out, c_out, h_out, mu_out, mi_out, y_ref, conf_ref, held_ref, start_ref,
                 y_send, c_send, h_send, mu_send, mi_send, w_ref, right_ref, v_ref, held_right_ref, x_all, x_own, f_own,
                 z_s, z_r, xy_s, xy_r, sib_s, sib_r, own_s, own_r, c_s, c_r, h_s, h_r, mu_s, mu_r, mi_s, mi_r,
                 xz_s, xz_r, xxy_s, xxy_r, xsib_s, xsib_r, f_s, f_r, local):
    zs = users // 2
    i, u, z, c = place(users, items)
    sibling = (2 * z + 1 - c, i)
    quarter = y_send.shape[2]
    user_peers = [lax.rem(u + k, users) for k in range(1, users)]
    item_peers = [lax.rem(i + e, items) for e in range(1, items)]
    neighbours = [(p, i) for p in user_peers] + [(u, p) for p in item_peers]
    loads = [
        pltpu.make_async_copy(y_hbm, y_ref, local.at[5]),
        pltpu.make_async_copy(held_hbm, held_ref, local.at[6]),
        pltpu.make_async_copy(conf_hbm, conf_ref, local.at[7]),
        pltpu.make_async_copy(start_hbm.at[:, u], start_ref, local.at[8]),
    ]
    for load in loads:
        load.start()
    greet(neighbours)
    describe(mu_send, ti_ref, tu_ref, tc_ref, w_ref.shape[0] // users)
    describe(mi_send, hu_ref, hi_ref, hc_ref, v_ref.shape[0] // items)
    loads[0].wait()
    for q in range(items):
        top, bottom = halves(y_ref[q * quarter:(q + 1) * quarter, :])
        y_send[q, 0] = top
        y_send[q, 1] = bottom
    await_greetings(neighbours)

    pending, tiled = [], []
    crossing = []
    for d in range(1, zs):
        peer = 2 * lax.rem(z + d, zs) + c
        crossing.append(send(y_send.at[i], y_out.at[u, i], z_s.at[d], z_r.at[d], (peer, i)))
    pending.append(send(y_send, y_out.at[u], own_s, own_r, sibling))
    keep = [pltpu.make_async_copy(y_send, y_out.at[u], local.at[0])]
    keep[0].start()

    held_slots = held_ref.shape[0]
    loads[1].wait()
    pack_rows(lambda s: held_ref[s].astype(jnp.float32), h_send, held_slots, items)
    for e, p in enumerate(item_peers):
        tiled.append(send(h_send.at[p], h_out.at[i], h_s.at[e], h_r.at[e], (u, p)))
        tiled.append(send(mi_send, mi_out.at[i], mi_s.at[e], mi_r.at[e], (u, p)))
    for k, p in enumerate(user_peers):
        tiled.append(send(mu_send, mu_out.at[u], mu_s.at[k], mu_r.at[k], (p, i)))
    slots = conf_ref.shape[0]
    loads[2].wait()
    pack_rows(lambda s: conf_ref[s].astype(jnp.float32).T, c_send, slots, users)
    for k, p in enumerate(user_peers):
        tiled.append(send(c_send.at[p], c_out.at[u], c_s.at[k], c_r.at[k], (p, i)))
    keep.append(pltpu.make_async_copy(c_send.at[u], c_out.at[u], local.at[1]))
    keep.append(pltpu.make_async_copy(h_send.at[i], h_out.at[i], local.at[2]))
    keep.append(pltpu.make_async_copy(mu_send, mu_out.at[u], local.at[3]))
    keep.append(pltpu.make_async_copy(mi_send, mi_out.at[i], local.at[4]))
    for copy in keep[1:]:
        copy.start()

    sent, stages = [], []
    for d in range(1, zs):
        shard = 2 * lax.rem(z - d + zs, zs) + c
        stages.append(exchange(
            items, u, i, d, lambda q, n=shard: y_out.at[n, q], lambda q, h, n=shard: y_out.at[n, q, h],
            sibling, xy_s, xy_r, sib_s, sib_r, sent, pending,
        ))
    for d in range(1, zs):
        crossing[d - 1].wait_recv()
        stages[d - 1][0](y_out.at[2 * lax.rem(z - d + zs, zs) + c, i])
    for stage in stages:
        stage[1]()
    for copy in tiled:
        copy.wait()
    for copy in keep:
        copy.wait()
    loads[3].wait()
    place_tiles(mu_out, c_out, w_ref, right_ref, w_ref.shape[0] // users)
    place_tiles(mi_out, h_out, v_ref, held_right_ref, v_ref.shape[0] // items)
    for stage in stages:
        stage[2]()
    for copy in crossing + sent:
        copy.wait_send()
    for copy in pending:
        copy.wait()

    _, blocks, part, rank = x_own.shape
    x = conjugate(
        lambda n: (merge_rows(y_out[n, :, 0]), merge_rows(y_out[n, :, 1])),
        w_ref, right_ref, start_ref[...].reshape(blocks * part, rank), blocks * part, rank, users,
    )
    top, bottom = halves(x)
    x_own[0] = top.astype(jnp.float32).reshape(blocks, part, rank).astype(jnp.bfloat16)
    x_own[1] = bottom.astype(jnp.float32).reshape(blocks, part, rank).astype(jnp.bfloat16)
    z_peers = [2 * lax.rem(z + d, zs) + c for d in range(1, zs)]
    crossing, sent, pending, stages = [], [], [], []
    own = x_all.at[i, :, :, u]
    for d, p in enumerate(z_peers):
        crossing.append(send(x_own, own, xz_s.at[d], xz_r.at[d], (p, i)))
    for d in range(zs):
        shard = 2 * lax.rem(z - d + zs, zs) + c
        stages.append(exchange(
            items, u, i, d, lambda q, n=shard: x_all.at[q, :, :, n], lambda q, h, n=shard: x_all.at[q, h, :, n],
            sibling, xxy_s, xxy_r, xsib_s, xsib_r, sent, pending,
        ))
    stages[0][0](x_own)
    keep = pltpu.make_async_copy(x_own, own, local.at[9])
    keep.start()
    for d in range(1, zs):
        crossing[d - 1].wait_recv()
        stages[d][0](x_all.at[i, :, :, 2 * lax.rem(z - d + zs, zs) + c])
    for number in (1, 2):
        for stage in stages:
            stage[number]()
    for copy in crossing + sent:
        copy.wait_send()
    for copy in pending:
        copy.wait()
    keep.wait()

    new_ref[...] = merge_rows(x_all[i, 0]).astype(jnp.float32) + merge_rows(x_all[i, 1]).astype(jnp.float32)
    held_blocks, held_part, _ = f_own.shape
    folded = conjugate(
        lambda n: (merge_rows(x_all[n, 0]), merge_rows(x_all[n, 1])),
        v_ref, held_right_ref, None, held_blocks * held_part, rank, items,
    )
    f_own[...] = folded.reshape(held_blocks, held_part, rank)
    mine = fold_ref.at[:, i]
    copies = [send(f_own, mine, f_s.at[e], f_r.at[e], (u, p)) for e, p in enumerate(item_peers)]
    last = pltpu.make_async_copy(f_own, mine, local.at[10])
    last.start()
    for copy in copies:
        copy.wait()
    last.wait()


def sweep(users, items, factors, conf, held, start, lists, held_lists):
    rows, rank = factors.shape
    slots, width = conf.shape[0], conf.shape[1]
    held_slots = held.shape[0]
    item_blocks, _, part, _ = start.shape
    user_blocks, held_blocks, held_part = rows // width, 2, width // items
    zs = users // 2
    y_piece = (2, rows // items, rank)
    c_piece, h_piece = (slots * part, width), (held_slots * held_part, width)
    bf16, f32, i32 = jnp.bfloat16, jnp.float32, jnp.int32
    item_side = (users * user_blocks, item_blocks * part, width)
    held_side = (items * item_blocks, held_blocks * held_part, width)
    dma = pltpu.SemaphoreType.DMA
    rounds = [dma((zs,)), dma((zs,))] + [dma((zs, items))] * 4
    return pl.pallas_call(
        functools.partial(sweep_kernel, users, items),
        out_shape=[
            jax.ShapeDtypeStruct((item_blocks * width, rank), f32),
            jax.ShapeDtypeStruct((held_blocks, items, held_part, rank), f32),
        ],
        in_specs=[HBM] * 4 + [SMEM] * 6,
        out_specs=[VMEM, VMEM],
        scratch_shapes=[
            pltpu.VMEM((users, items) + y_piece, bf16),
            pltpu.VMEM((users,) + c_piece, bf16),
            pltpu.VMEM((items,) + h_piece, bf16),
            pltpu.VMEM((users, slots, width), i32),
            pltpu.VMEM((items, held_slots, width), i32),
            pltpu.VMEM((rows, rank), f32),
            pltpu.VMEM(conf.shape, bf16),
            pltpu.VMEM(held.shape, bf16),
            pltpu.VMEM((item_blocks, part, rank), f32),
            pltpu.VMEM((items,) + y_piece, bf16),
            pltpu.VMEM((users,) + c_piece, bf16),
            pltpu.VMEM((items,) + h_piece, bf16),
            pltpu.VMEM((slots, width), i32),
            pltpu.VMEM((held_slots, width), i32),
            pltpu.VMEM(item_side, f32),
            pltpu.VMEM(item_side, f32),
            pltpu.VMEM(held_side, f32),
            pltpu.VMEM(held_side, f32),
            pltpu.VMEM((items, 2, item_blocks, users, part, rank), bf16),
            pltpu.VMEM((2, item_blocks, part, rank), bf16),
            pltpu.VMEM((held_blocks, held_part, rank), f32),
        ] + rounds + [dma, dma, dma((users,)), dma((users,)), dma((items,)), dma((items,)),
                      dma((users,)), dma((users,)), dma((items,)), dma((items,))]
        + rounds + [dma((items,)), dma((items,)), dma((11,))],
        compiler_params=pltpu.CompilerParams(
            collective_id=0, has_side_effects=True, vmem_limit_bytes=60 * 2**20
        ),
        name="sweep",
    )(factors, conf, held, start, *lists, *held_lists)


def shards(user_factors, item_factors, tile_user, tile_item, tile_count, tile_conf,
           held_user, held_item, held_count, held_conf):
    users, items = lax.axis_size("user"), lax.axis_size("item")
    width = tile_conf.shape[-1]
    rank = user_factors.shape[1]
    new_items, folded = sweep(
        users, items, user_factors,
        tile_conf.reshape(-1, width, width), held_conf.reshape(-1, width, width),
        item_factors.reshape(item_factors.shape[0] // width, users, width // users, rank),
        (tile_item[0, 0].T, tile_user[0, 0].T, tile_count[0]),
        (held_user[0, 0].T, held_item[0, 0].T, held_count[0]),
    )
    return new_items, folded.reshape(-1, rank)


def solution(mesh):
    in_specs = (
        P("user", None),
        P("item", None),
        P("item", "user", None, None),
        P("item", "user", None, None),
        P("item", "user", None),
        P("item", "user", None, None, None, None),
        P("user", "item", None, None),
        P("user", "item", None, None),
        P("user", "item", None),
        P("user", "item", None, None, None, None),
    )
    out_specs = (P("item", None), P("user", None))
    return jax.shard_map(shards, mesh=mesh, in_specs=in_specs, out_specs=out_specs, check_vma=False)
```
